32 devices in a mesh: groups: 2 (over x), fsdp: 8 (over z, y), tenant: 2 (over core).
Axes of the slice: x: 2, y: 2, z: 4, core: 2. Of those that a mesh axis runs over, the one named last changes fastest.
Arguments:
- tokens: bfloat16 [4096, 8192], P(('groups', 'fsdp', 'tenant')), parts along dimension 0, may hold values from -6 to 6
- grad_out: bfloat16 [4096, 1024], P(('groups', 'fsdp', 'tenant')), parts along dimension 0, may hold values from -6 to 6
- base_weight: bfloat16 [8192, 1024], P('fsdp'), may hold values from -0.0625 to 0.0625
- page_a: bfloat16 [32, 128, 8192], P(('groups', 'fsdp', 'tenant')), parts along dimension 0, may hold values from -0.0625 to 0.0625
- page_b: bfloat16 [32, 128, 1024], P(('groups', 'fsdp', 'tenant')), parts along dimension 0, may hold values from -0.5 to 0.5
- page_owner: int32 [32], P('groups'), parts along dimension 0, may hold values from 0 to 15, as said below
- row_tenant: int32 [4096], P(('groups', 'fsdp', 'tenant')), parts along dimension 0, may hold values from 0 to 63, as said below
Outputs:
- projected: bfloat16 [4096, 1024], P(('groups', 'fsdp', 'tenant')), parts along dimension 0
- grad_tokens: bfloat16 [4096, 8192], P(('groups', 'fsdp', 'tenant')), parts along dimension 0
- grad_page_a: bfloat16 [32, 128, 8192], P(('groups', 'fsdp', 'tenant')), parts along dimension 0
- grad_page_b: bfloat16 [32, 128, 1024], P(('groups', 'fsdp', 'tenant')), parts along dimension 0
The draws below stay inside these ranges and needn't reach their ends.
There are 2 independent parts, one for each index of `groups`. The reference program is written for one: setup_inputs(seed, part) draws one part's arguments, and reference() takes and returns one part's arrays. A program takes and returns all parts, laid end to end along the dimension named above; an argument that names none is the same for every part. Nothing has to cross between parts.
Inputs may be any that keep to these rules, and one draw needn't show every extreme that they name: A permutation: page p is stored at position page_owner[p] of page_a and page_b, that is on that device of fsdp+tenant. `row_tenant`: among the 128 rows of one device, at most 10 name tenants of any one page; some page gets exactly 10 rows from every device.
All inputs are finite; a program needn't handle non-finite values.
Results may differ from the reference program's by a relative error of at most 0.0051.
Values may be sent and summed in bfloat16 or wider, within the bound.
No kernel may reach another device: no remote copies, remote signals or barrier semaphores. Data moves between devices by JAX's collectives and lax.ppermute only.
A program may use at most 128 MiB of HBM per device.

```python
import jax
import jax.numpy as jnp
from jax import lax

D = 8192
KVW = 1024
RANK = 32
PAGE_ROWS = 128
ROWS_DEV = 128
PAGES = 16
CAP = 10
TOKENS = 2048
N_FSDP = 8
N_TENANT = 2


def owner_table(key):
    return jax.random.permutation(jax.random.fold_in(key, 11), PAGES).astype(jnp.int32)


def draw_page_owner(key, part):
    table = owner_table(key)
    return table


def draw_row_tenant(key, part):
    table = owner_table(key)
    key = jax.random.fold_in(key, 2)
    devices = N_FSDP * N_TENANT
    slots = devices * CAP
    per_page = PAGE_ROWS // RANK
    keys = jax.random.split(key, 5)
    popular = jax.random.randint(keys[0], (devices,), 0, 4)
    hottest = jax.random.randint(keys[1], (), 0, devices)
    popular = jnp.where(jnp.arange(devices) == hottest, 4, popular)
    noise = jax.random.randint(keys[2], (devices, slots), 0, 65536)
    owner_of_slot = jnp.arange(slots, dtype=jnp.int32) // CAP
    score = (popular[owner_of_slot][None, :] * 65536 + noise) * slots + jnp.arange(slots, dtype=jnp.int32)[None, :]
    chosen = jnp.argsort(-score, axis=1)[:, :ROWS_DEV]
    mixing = jax.random.randint(keys[3], (devices, ROWS_DEV), 0, 65536) * ROWS_DEV + jnp.arange(ROWS_DEV, dtype=jnp.int32)[None, :]
    shuffled = jnp.take_along_axis(chosen, jnp.argsort(mixing, axis=1), axis=1)
    target = (shuffled // CAP).astype(jnp.int32)
    stored_page = jnp.argsort(table).astype(jnp.int32)
    member = jax.random.randint(keys[4], (devices, ROWS_DEV), 0, per_page)
    tenant = stored_page[target] * per_page + member
    return tenant.reshape(-1).astype(jnp.int32)


def shard_levels(stream_key, shape, cuts, least, largest):
    factor_of = 1.0
    for axis_at, parts in cuts:
        steps = jax.random.uniform(jax.random.fold_in(jax.random.fold_in(stream_key, 6), axis_at), (parts,), jnp.float32, least / len(cuts), largest / len(cuts))
        factor_of = factor_of * jnp.repeat(jnp.exp(steps), shape[axis_at] // parts).reshape((-1,) + (1,) * (len(shape) - 1 - axis_at))
    return factor_of


def normal_values(own_key, extent, spread, limit, cuts=(), kind=jnp.bfloat16):
    factor_of = shard_levels(own_key, extent, cuts, -0.22, 0.18) if cuts else 1.0
    entries = jax.random.normal(own_key, extent, jnp.float32) * spread * factor_of
    return jnp.minimum(jnp.maximum(entries, -limit), limit).astype(kind)


def setup_inputs(seed: int = 0, part: int = 0) -> dict:
    arg_keys = jax.random.split(jax.random.key(seed), 8)
    part_keys = jax.random.split(jax.random.fold_in(arg_keys[7], part), 8)
    return {
        "tokens": normal_values(part_keys[0], (TOKENS, D), 1.0, 6.0, ((0, 16),)),
        "grad_out": normal_values(part_keys[1], (TOKENS, KVW), 1.0, 6.0, ((0, 16),)),
        "base_weight": normal_values(arg_keys[2], (D, KVW), D ** -0.5, 0.0625, ((0, 8),)),
        "page_a": normal_values(part_keys[3], (PAGES, PAGE_ROWS, D), D ** -0.5, 0.0625, ((0, 16),)),
        "page_b": normal_values(part_keys[4], (PAGES, PAGE_ROWS, KVW), PAGE_ROWS ** -0.5, 0.5, ((0, 16),)),
        "page_owner": draw_page_owner(jax.random.fold_in(jax.random.fold_in(arg_keys[7], part), 71), part),
        "row_tenant": draw_row_tenant(jax.random.fold_in(jax.random.fold_in(arg_keys[7], part), 71), part),
    }


adapter_scale = 2.0


def reference(tokens, grad_out, base_weight, page_a, page_b, page_owner, row_tenant):
    devices = N_FSDP * N_TENANT
    slots = devices * CAP
    per_page = PAGE_ROWS // RANK
    target = page_owner[row_tenant // per_page].astype(jnp.int32)
    member = row_tenant % per_page
    padded_tok = jnp.concatenate([tokens, jnp.zeros((1, D), jnp.bfloat16)], axis=0)
    padded_grad = jnp.concatenate([grad_out, jnp.zeros((1, KVW), jnp.bfloat16)], axis=0)
    padded_member = jnp.concatenate([member, jnp.full((1,), -1, jnp.int32)], axis=0)
    block_of_col = (jnp.arange(PAGE_ROWS, dtype=jnp.int32) // RANK)

    def per_store(place):
        index = jnp.nonzero(target == place, size=slots, fill_value=TOKENS)[0].astype(jnp.int32)
        token_rows = padded_tok[index]
        row_gradient = padded_grad[index]
        which = padded_member[index]
        mask = (which[:, None] == block_of_col[None, :]).astype(jnp.float32)
        left_factor = page_a[place]
        right_factor = page_b[place]
        reduced_rank_rows = (lax.dot_general(token_rows, left_factor, (((1,), (1,)), ((), ())), preferred_element_type=jnp.float32) * mask).astype(jnp.bfloat16)
        adapter_output = (adapter_scale * jnp.dot(reduced_rank_rows, right_factor, preferred_element_type=jnp.float32)).astype(jnp.bfloat16)
        reduced_gradient = (lax.dot_general(row_gradient, right_factor, (((1,), (1,)), ((), ())), preferred_element_type=jnp.float32) * mask).astype(jnp.bfloat16)
        adapter_backward = (adapter_scale * jnp.dot(reduced_gradient, left_factor, preferred_element_type=jnp.float32)).astype(jnp.bfloat16)
        left_factor_gradient = (adapter_scale * lax.dot_general(reduced_gradient, token_rows, (((0,), (0,)), ((), ())), preferred_element_type=jnp.float32)).astype(jnp.bfloat16)
        right_factor_gradient = (adapter_scale * lax.dot_general(reduced_rank_rows, row_gradient, (((0,), (0,)), ((), ())), preferred_element_type=jnp.float32)).astype(jnp.bfloat16)
        return index, adapter_output, adapter_backward, left_factor_gradient, right_factor_gradient

    index, adapter_output, adapter_backward, left_factor_gradient, right_factor_gradient = lax.map(per_store, jnp.arange(devices, dtype=jnp.int32))
    flat = index.reshape(-1)
    out_rows = jnp.zeros((TOKENS + 1, KVW), jnp.bfloat16).at[flat].set(adapter_output.reshape(-1, KVW))[:TOKENS]
    back_rows = jnp.zeros((TOKENS + 1, D), jnp.bfloat16).at[flat].set(adapter_backward.reshape(-1, D))[:TOKENS]
    base_out = jnp.dot(tokens, base_weight, preferred_element_type=jnp.float32)
    projected = (base_out + out_rows.astype(jnp.float32)).astype(jnp.bfloat16)
    base_back = lax.dot_general(grad_out, base_weight, (((1,), (1,)), ((), ())), preferred_element_type=jnp.float32)
    grad_tokens = (base_back + back_rows.astype(jnp.float32)).astype(jnp.bfloat16)
    return projected, grad_tokens, left_factor_gradient, right_factor_gradient
```

```python
import functools

import jax
import jax.numpy as jnp
from jax import lax
from jax.experimental import pallas as pl
from jax.experimental.pallas import tpu as pltpu
from jax.sharding import PartitionSpec as P

RANK = 32
CHUNKS = 8
VMEM_LIMIT = 48 * 1024 * 1024

adapter_scale = 2.0

F32 = jnp.float32
BF16 = jnp.bfloat16
NT = (((1,), (1,)), ((), ()))
TN = (((0,), (0,)), ((), ()))


def iota(shape, dim):
    return lax.broadcasted_iota(jnp.int32, shape, dim)


def piece_and_slot(index, cap):
    piece = jnp.zeros_like(index)
    for k in range(1, CHUNKS + 1):
        piece = piece + (index >= k * cap).astype(jnp.int32)
    return piece, index - piece * cap


def spread_mask(rows, cap, lanes):
    block = CHUNKS * cap
    piece, _ = piece_and_slot(iota((block, CHUNKS * lanes), 0), cap)
    group = jnp.zeros_like(piece)
    lane = iota(piece.shape, 1)
    for k in range(1, CHUNKS):
        group = group + (lane >= k * lanes).astype(jnp.int32)
    mask = (piece == group).astype(F32).astype(BF16)
    return jnp.concatenate([mask] * (rows // block), axis=0)


def spread(rows, cap):
    return jnp.concatenate([rows] * CHUNKS, axis=1) * spread_mask(
        rows.shape[0], cap, rows.shape[1]
    )


def pick_piece(wide, cap, height, lanes):
    n = wide.shape[0]
    piece, _ = piece_and_slot(iota((height, lanes), 0), cap)
    piece = jnp.concatenate([piece] * (n // height), axis=0)
    total = jnp.zeros((n, lanes), F32)
    for k in range(CHUNKS):
        total = total + jnp.where(piece == k, wide[:, k * lanes : (k + 1) * lanes], 0.0)
    return total


def same_slot(cap, columns):
    shape = (CHUNKS * cap, columns)
    _, slot = piece_and_slot(iota(shape, 0), cap)
    piece_c, slot_c = piece_and_slot(iota(shape, 1), cap)
    return ((slot == slot_c) & (piece_c < CHUNKS)).astype(F32)


def mask_of_slot(cap, columns):
    shape = (CHUNKS * cap, columns)
    _, slot = piece_and_slot(iota(shape, 0), cap)
    return (iota(shape, 1) == CHUNKS * cap + slot).astype(F32)


def load_pieces(src, dst, sem, height, width):
    copies = [
        pltpu.make_async_copy(
            src.at[:, pl.ds(k * width, width)], dst.at[pl.ds(k * height, height), :], sem.at[k]
        )
        for k in range(CHUNKS)
    ]
    for copy in copies:
        copy.start()
    for copy in copies:
        copy.wait()


def route_kernel(
    devices, cap, per_page, owner_ref, tenant_ref, grads_ref, send_ref, row_ref, col_ref
):
    rows = tenant_ref.shape[1]
    block = CHUNKS * cap
    height = send_ref.shape[1]
    width = send_ref.shape[2]
    tenant = tenant_ref[...]
    page = tenant // per_page
    member = tenant - page * per_page

    def add_page(p, target):
        return target + jnp.where(page == p, owner_ref[p], 0)

    target = lax.fori_loop(0, owner_ref.shape[0], add_page, jnp.zeros_like(page))
    chosen = (iota((devices, rows), 0) == target).astype(F32)
    earlier = (iota((rows, rows), 0) < iota((rows, rows), 1)).astype(F32)
    before = jnp.dot(chosen.astype(BF16), earlier.astype(BF16), preferred_element_type=F32)
    slot = target.astype(F32) * cap + jnp.sum(before * chosen, axis=0, keepdims=True)
    row_ref[...] = slot
    col_ref[...] = jnp.transpose(jnp.broadcast_to(slot, (rows, rows)))

    member_mask = (iota((width, rows), 0) // RANK == member).astype(F32).astype(BF16)
    pieces = jnp.concatenate(
        [grads_ref[:, k * width : (k + 1) * width] for k in range(CHUNKS)], axis=0
    )
    _, slot_of = piece_and_slot(iota((block, rows), 0), cap)
    tail = iota((height - block, rows), 0)
    tail = jnp.where(tail < cap, tail, -(10**6))
    for d in range(devices):
        here = (slot == (slot_of + d * cap).astype(F32)).astype(F32).astype(BF16)
        send_ref[d, 0:block, :] = jnp.dot(
            spread(here, cap), pieces, preferred_element_type=F32
        ).astype(BF16)
        here = (slot == (tail + d * cap).astype(F32)).astype(F32).astype(BF16)
        send_ref[d, block:height, :] = lax.dot_general(
            here, member_mask, NT, preferred_element_type=F32
        ).astype(BF16)


def dispatch_kernel(cap, slot_ref, tokens_ref, out_ref, pieces, sem):
    step = pl.program_id(0)
    rows = slot_ref.shape[1]
    width = pieces.shape[1]
    block = CHUNKS * cap

    @pl.when(step == 0)
    def _():
        load_pieces(tokens_ref, pieces, sem, rows, width)

    group = out_ref.shape[0] // block
    _, slot_of = piece_and_slot(iota((block, rows), 0), cap)
    slot = slot_ref[...]
    here = jnp.concatenate(
        [
            (slot == (slot_of + (step * group + d) * cap).astype(F32)).astype(F32).astype(BF16)
            for d in range(group)
        ],
        axis=0,
    )
    out_ref[...] = jnp.dot(spread(here, cap), pieces[...], preferred_element_type=F32).astype(BF16)


def back_kernel(cap, got_ref, b_ref, a_ref, back_ref, rank_ref, mask_ref, pieces, sem):
    step = pl.program_id(0)
    ranks = b_ref.shape[0]
    group, height, width = got_ref.shape
    block = CHUNKS * cap

    @pl.when(step == 0)
    def _():
        load_pieces(a_ref, pieces, sem, ranks, pieces.shape[1])

    b_pieces = jnp.concatenate(
        [b_ref[:, k * width : (k + 1) * width] for k in range(CHUNKS)], axis=0
    )
    fold = same_slot(cap, height)
    member = mask_of_slot(cap, height).astype(BF16)
    ranks_of = []
    for d in range(group):
        got = got_ref[d]
        wide = lax.dot_general(got, b_pieces, NT, preferred_element_type=F32)
        part = pick_piece(wide, cap, height, ranks)
        full = jnp.dot(fold, part, precision=lax.Precision.HIGHEST, preferred_element_type=F32)
        mask = jnp.dot(member, got, preferred_element_type=F32)
        ranks_of.append((full * mask).astype(BF16))
        mask_ref[d * block : (d + 1) * block, :] = mask.astype(BF16)
    rank_rows = jnp.concatenate(ranks_of, axis=0)
    rank_ref[...] = rank_rows
    back_ref[...] = (
        adapter_scale * jnp.dot(spread(rank_rows, cap), pieces[...], preferred_element_type=F32)
    ).astype(BF16)


def forth_kernel(cap, got_ref, mask_ref, a_ref, b_ref, out_ref, rank_ref, pieces, sem):
    step = pl.program_id(0)
    ranks = b_ref.shape[0]
    block = CHUNKS * cap
    width = out_ref.shape[1]
    group = got_ref.shape[0] // block

    @pl.when(step == 0)
    def _():
        load_pieces(a_ref, pieces, sem, ranks, pieces.shape[1])

    b_pieces = jnp.concatenate(
        [b_ref[:, k * width : (k + 1) * width] for k in range(CHUNKS)], axis=0
    )
    wide = lax.dot_general(got_ref[...], pieces[...], NT, preferred_element_type=F32)
    part = pick_piece(wide, cap, block, ranks)
    fold = same_slot(cap, block)
    full = jnp.concatenate(
        [
            jnp.dot(
                fold,
                part[d * block : (d + 1) * block, :],
                precision=lax.Precision.HIGHEST,
                preferred_element_type=F32,
            )
            for d in range(group)
        ],
        axis=0,
    )
    rank_rows = (full * mask_ref[...].astype(F32)).astype(BF16)
    rank_ref[...] = rank_rows
    out_ref[...] = (
        adapter_scale * jnp.dot(spread(rank_rows, cap), b_pieces, preferred_element_type=F32)
    ).astype(BF16)


def page_grad_kernel(cap, tok_ref, grad_ref, low_ref, rank_ref, ga_ref, gb_ref):
    ranks = rank_ref.shape[1]
    block = CHUNKS * cap
    wide = tok_ref.shape[1]
    narrow = grad_ref.shape[2]
    left = lax.dot_general(
        spread(rank_ref[...], cap), tok_ref[...], TN, preferred_element_type=F32
    )
    grads = jnp.concatenate(
        [grad_ref[d, 0:block, :] for d in range(grad_ref.shape[0])], axis=0
    )
    right = lax.dot_general(spread(low_ref[...], cap), grads, TN, preferred_element_type=F32)
    for k in range(CHUNKS):
        ga_ref[:, k * wide : (k + 1) * wide] = (
            adapter_scale * left[k * ranks : (k + 1) * ranks, :]
        ).astype(BF16)
        gb_ref[:, k * narrow : (k + 1) * narrow] = (
            adapter_scale * right[k * ranks : (k + 1) * ranks, :]
        ).astype(BF16)


def base_kernel(tok_ref, grad_ref, w_ref, out_ref, back_ref):
    @pl.when(pl.program_id(0) == 0)
    def _():
        out_ref[...] = jnp.zeros_like(out_ref)

    weight = w_ref[...]
    out_ref[...] += jnp.dot(tok_ref[...], weight, preferred_element_type=F32)
    back_ref[...] = lax.dot_general(grad_ref[...], weight, NT, preferred_element_type=F32)


def own_slots(col, cap, total, piece):
    block = CHUNKS * cap
    rows = col.shape[0]
    piece_of, slot_of = piece_and_slot(iota((rows, block), 1), cap)
    key = jnp.where(piece_of == piece, slot_of, -(10**6))
    parts = []
    for d in range(total // block):
        parts.append((col == (key + d * cap).astype(F32)).astype(F32).astype(BF16))
    return jnp.concatenate(parts, axis=1)


def combine_back_kernel(cap, col_ref, got_ref, base_ref, out_ref):
    here = own_slots(col_ref[:, 0:1], cap, got_ref.shape[0], pl.program_id(0))
    rows = jnp.dot(here, got_ref[...], preferred_element_type=F32)
    out_ref[...] = (base_ref[...] + rows).astype(BF16)


def combine_out_kernel(cap, col_ref, got_ref, base_ref, out_ref):
    width = got_ref.shape[1]
    for k in range(CHUNKS):
        here = own_slots(col_ref[:, 0:1], cap, got_ref.shape[0], k)
        rows = jnp.dot(here, got_ref[...], preferred_element_type=F32)
        at = slice(k * width, (k + 1) * width)
        out_ref[:, at] = (base_ref[:, at] + rows).astype(BF16)


def whole(shape):
    return pl.BlockSpec(shape, lambda *_: (0,) * len(shape))


def params(semantics=None):
    return pltpu.CompilerParams(vmem_limit_bytes=VMEM_LIMIT, dimension_semantics=semantics)


def cost(flops, nbytes):
    return pl.CostEstimate(flops=int(flops), bytes_accessed=int(nbytes), transcendentals=0)


def on_device(tokens, grad_out, base_weight, page_a, page_b, page_owner, row_tenant):
    rows, width = tokens.shape
    narrow = grad_out.shape[1]
    fsdp_size = lax.axis_size("fsdp")
    tenant_size = lax.axis_size("tenant")
    group_size = lax.axis_size("groups")
    devices = fsdp_size * tenant_size
    cap = max(4, 4 * rows // (3 * devices))
    per_page = page_a.shape[1] // RANK
    ranks = page_a.shape[1]
    block = CHUNKS * cap
    total = devices * block
    height = block + -(-cap // 16) * 16
    wp, np_ = width // CHUNKS, narrow // CHUNKS
    left_factor, right_factor = page_a[0], page_b[0]
    axes = ("fsdp", "tenant")

    def exchange(x):
        return lax.all_to_all(x, axes, split_axis=0, concat_axis=0, tiled=True)

    any_spec = pl.BlockSpec(memory_space=pl.ANY)

    shares = group_size * tenant_size
    share = base_weight.shape[0] // shares
    which = lax.axis_index("groups") * tenant_size + lax.axis_index("tenant")
    mine = lax.dynamic_slice_in_dim(base_weight, which * share, share, 0)
    weight = lax.all_gather(mine, ("fsdp", "groups", "tenant"), axis=0, tiled=True)

    send_grads, slot_row, slot_col = pl.pallas_call(
        functools.partial(route_kernel, devices, cap, per_page),
        out_shape=(
            jax.ShapeDtypeStruct((devices, height, np_), BF16),
            jax.ShapeDtypeStruct((1, rows), F32),
            jax.ShapeDtypeStruct((rows, rows), F32),
        ),
        in_specs=[
            pl.BlockSpec(memory_space=pltpu.SMEM),
            pl.BlockSpec(memory_space=pltpu.VMEM),
            pl.BlockSpec(memory_space=pltpu.VMEM),
        ],
        out_specs=tuple(pl.BlockSpec(memory_space=pltpu.VMEM) for _ in range(3)),
        compiler_params=params(),
        cost_estimate=cost(2 * total * rows * narrow, 2 * total * np_ * 2),
        name="route",
    )(page_owner, row_tenant.reshape(1, rows), grad_out)
    got_grads = exchange(send_grads)

    steps = 4 if devices % 4 == 0 else 1
    part = total // steps
    send_tokens = pl.pallas_call(
        functools.partial(dispatch_kernel, cap),
        out_shape=jax.ShapeDtypeStruct((total, wp), BF16),
        grid=(steps,),
        in_specs=[whole((1, rows)), any_spec],
        out_specs=pl.BlockSpec((part, wp), lambda i: (i, 0)),
        scratch_shapes=[
            pltpu.VMEM((CHUNKS * rows, wp), BF16),
            pltpu.SemaphoreType.DMA((CHUNKS,)),
        ],
        compiler_params=params(("arbitrary",)),
        cost_estimate=cost(2 * total * rows * width, 2 * (total * wp + rows * width)),
        name="dispatch",
    )(slot_row, tokens)
    got_tokens = exchange(send_tokens.reshape(devices, block, wp)).reshape(total, wp)

    back, rank_rows, mask_rows = pl.pallas_call(
        functools.partial(back_kernel, cap),
        out_shape=(
            jax.ShapeDtypeStruct((total, wp), BF16),
            jax.ShapeDtypeStruct((total, ranks), BF16),
            jax.ShapeDtypeStruct((total, ranks), BF16),
        ),
        grid=(steps,),
        in_specs=[
            pl.BlockSpec((devices // steps, height, np_), lambda i: (i, 0, 0)),
            whole((ranks, narrow)),
            any_spec,
        ],
        out_specs=(
            pl.BlockSpec((part, wp), lambda i: (i, 0)),
            pl.BlockSpec((part, ranks), lambda i: (i, 0)),
            pl.BlockSpec((part, ranks), lambda i: (i, 0)),
        ),
        scratch_shapes=[
            pltpu.VMEM((CHUNKS * ranks, wp), BF16),
            pltpu.SemaphoreType.DMA((CHUNKS,)),
        ],
        compiler_params=params(("arbitrary",)),
        cost_estimate=cost(2 * total * ranks * width, 2 * (total * wp + ranks * width)),
        name="rank_grad_back",
    )(got_grads, right_factor, left_factor)
    got_back = exchange(back.reshape(devices, block, wp)).reshape(total, wp)

    out_packed, low_rows = pl.pallas_call(
        functools.partial(forth_kernel, cap),
        out_shape=(
            jax.ShapeDtypeStruct((total, np_), BF16),
            jax.ShapeDtypeStruct((total, ranks), BF16),
        ),
        grid=(steps,),
        in_specs=[
            pl.BlockSpec((part, wp), lambda i: (i, 0)),
            pl.BlockSpec((part, ranks), lambda i: (i, 0)),
            any_spec,
            whole((ranks, narrow)),
        ],
        out_specs=(
            pl.BlockSpec((part, np_), lambda i: (i, 0)),
            pl.BlockSpec((part, ranks), lambda i: (i, 0)),
        ),
        scratch_shapes=[
            pltpu.VMEM((CHUNKS * ranks, wp), BF16),
            pltpu.SemaphoreType.DMA((CHUNKS,)),
        ],
        compiler_params=params(("arbitrary",)),
        cost_estimate=cost(2 * total * ranks * width, 2 * (total * wp + ranks * width)),
        name="lowrank_out",
    )(got_tokens, mask_rows, left_factor, right_factor)
    got_out = exchange(out_packed.reshape(devices, block, np_)).reshape(total, np_)

    grad_a, grad_b = pl.pallas_call(
        functools.partial(page_grad_kernel, cap),
        out_shape=(
            jax.ShapeDtypeStruct((ranks, width), BF16),
            jax.ShapeDtypeStruct((ranks, narrow), BF16),
        ),
        compiler_params=params(),
        cost_estimate=cost(2 * total * ranks * width, 2 * (total * wp + ranks * width)),
        name="page_grads",
    )(got_tokens, got_grads, low_rows, rank_rows)

    base_out, base_back = pl.pallas_call(
        base_kernel,
        out_shape=(
            jax.ShapeDtypeStruct((rows, narrow), F32),
            jax.ShapeDtypeStruct((rows, width), F32),
        ),
        grid=(CHUNKS,),
        in_specs=[
            pl.BlockSpec((rows, wp), lambda i: (0, i)),
            whole((rows, narrow)),
            pl.BlockSpec((wp, narrow), lambda i: (i, 0)),
        ],
        out_specs=(whole((rows, narrow)), pl.BlockSpec((rows, wp), lambda i: (0, i))),
        compiler_params=params(("arbitrary",)),
        cost_estimate=cost(4 * rows * width * narrow, 2 * width * narrow),
        name="base",
    )(tokens, grad_out, weight)

    projected = pl.pallas_call(
        functools.partial(combine_out_kernel, cap),
        out_shape=jax.ShapeDtypeStruct((rows, narrow), BF16),
        compiler_params=params(),
        cost_estimate=cost(2 * rows * total * narrow, 2 * total * np_),
        name="combine_out",
    )(slot_col, got_out, base_out)

    grad_tokens = pl.pallas_call(
        functools.partial(combine_back_kernel, cap),
        out_shape=jax.ShapeDtypeStruct((rows, width), BF16),
        grid=(CHUNKS,),
        in_specs=[
            whole((rows, rows)),
            whole((total, wp)),
            pl.BlockSpec((rows, wp), lambda i: (0, i)),
        ],
        out_specs=pl.BlockSpec((rows, wp), lambda i: (0, i)),
        compiler_params=params(("arbitrary",)),
        cost_estimate=cost(2 * rows * total * width, 2 * total * wp + 6 * rows * width),
        name="combine_back",
    )(slot_col, got_back, base_back)

    return projected, grad_tokens, grad_a[None], grad_b[None]


def solution(mesh):
    rows = P(("groups", "fsdp", "tenant"), None)
    pages = P(("groups", "fsdp", "tenant"), None, None)
    return jax.shard_map(
        on_device,
        mesh=mesh,
        in_specs=(
            rows,
            rows,
            P("fsdp", None),
            pages,
            pages,
            P("groups"),
            P(("groups", "fsdp", "tenant")),
        ),
        out_specs=(rows, rows, pages, pages),
        check_vma=False,
    )
```

```python
import functools

import jax
import jax.numpy as jnp
from jax import lax
from jax.experimental import pallas as pl
from jax.experimental.pallas import tpu as pltpu
from jax.sharding import PartitionSpec as P

RANK = 32
CHUNKS = 8
VMEM_LIMIT = 48 * 1024 * 1024

adapter_scale = 2.0

F32 = jnp.float32
BF16 = jnp.bfloat16
NT = (((1,), (1,)), ((), ()))
TN = (((0,), (0,)), ((), ()))


def iota(shape, dim):
    return lax.broadcasted_iota(jnp.int32, shape, dim)


def piece_and_slot(index, cap):
    piece = jnp.zeros_like(index)
    for k in range(1, CHUNKS + 1):
        piece = piece + (index >= k * cap).astype(jnp.int32)
    return piece, index - piece * cap


def spread_mask(rows, cap, lanes):
    block = CHUNKS * cap
    piece, _ = piece_and_slot(iota((block, CHUNKS * lanes), 0), cap)
    group = jnp.zeros_like(piece)
    lane = iota(piece.shape, 1)
    for k in range(1, CHUNKS):
        group = group + (lane >= k * lanes).astype(jnp.int32)
    mask = (piece == group).astype(F32).astype(BF16)
    return jnp.concatenate([mask] * (rows // block), axis=0)


def spread(rows, cap):
    return jnp.concatenate([rows] * CHUNKS, axis=1) * spread_mask(
        rows.shape[0], cap, rows.shape[1]
    )


def pick_piece(wide, cap, lanes):
    block, n = CHUNKS * cap, wide.shape[0]
    piece, _ = piece_and_slot(iota((block, lanes), 0), cap)
    piece = jnp.concatenate([piece] * (n // block), axis=0)
    total = jnp.zeros((n, lanes), F32)
    for k in range(CHUNKS):
        total = total + jnp.where(piece == k, wide[:, k * lanes : (k + 1) * lanes], 0.0)
    return total


def same_slot(cap):
    shape = (CHUNKS * cap, CHUNKS * cap)
    _, slot = piece_and_slot(iota(shape, 0), cap)
    _, slot_c = piece_and_slot(iota(shape, 1), cap)
    return (slot == slot_c).astype(F32)


def load_pieces(src, dst, sem, height, stride, start, width):
    return [
        pltpu.make_async_copy(
            src.at[:, pl.ds(k * stride + start, width)],
            dst.at[pl.ds(k * height, height), pl.ds(0, width)],
            sem.at[k],
        )
        for k in range(CHUNKS)
    ]


def start_all(copies):
    for copy in copies:
        copy.start()


def wait_all(copies):
    for copy in copies:
        copy.wait()


def rows_of_slots(slot, cap, first, group):
    _, slot_of = piece_and_slot(iota((CHUNKS * cap, slot.shape[1]), 0), cap)
    return jnp.concatenate(
        [
            (slot == (slot_of + (first + d) * cap).astype(F32)).astype(F32).astype(BF16)
            for d in range(group)
        ],
        axis=0,
    )


def earlier_rows(rows):
    return (iota((rows, rows), 0) < iota((rows, rows), 1)).astype(F32).astype(BF16)


def join(ref, first, group, block, start, count):
    return jnp.concatenate(
        [
            jnp.concatenate(
                [ref[d, (start + n) * block : (start + n + 1) * block, :] for n in range(count)],
                axis=1,
            )
            for d in range(first, first + group)
        ],
        axis=0,
    )


def route_kernel(
    devices, cap, per_page, owner_ref, tenant_ref, tokens_ref, grads_ref,
    send_ref, row_ref, col_ref, pieces, sem,
):
    step = pl.program_id(0)
    rows = tenant_ref.shape[1]
    group, height, lanes = send_ref.shape
    block = CHUNKS * cap
    half = pieces.shape[1] - lanes
    page = tenant_ref[...] // per_page
    member = tenant_ref[...] - page * per_page

    @pl.when(step == 0)
    def _():
        copies = load_pieces(tokens_ref, pieces, sem, rows, 2 * half, 0, half)
        copies += [
            pltpu.make_async_copy(
                grads_ref.at[:, pl.ds(k * lanes, lanes)],
                pieces.at[pl.ds(k * rows, rows), pl.ds(half, lanes)],
                sem.at[CHUNKS + k],
            )
            for k in range(CHUNKS)
        ]
        start_all(copies)

        def add_page(p, target):
            return target + jnp.where(page == p, owner_ref[p], 0)

        target = lax.fori_loop(0, owner_ref.shape[0], add_page, jnp.zeros_like(page))
        chosen = (iota((devices, rows), 0) == target).astype(F32)
        before = jnp.dot(chosen.astype(BF16), earlier_rows(rows), preferred_element_type=F32)
        slot = target.astype(F32) * cap + jnp.sum(before * chosen, axis=0, keepdims=True)
        row_ref[...] = slot
        col_ref[...] = jnp.transpose(jnp.broadcast_to(slot, (rows, rows)))
        wait_all(copies)

    slot = row_ref[...]
    here = spread(rows_of_slots(slot, cap, step * group, group), cap)
    packed = jnp.dot(here, pieces[...], preferred_element_type=F32).astype(BF16)
    of_member = (iota((lanes, rows), 0) // RANK == member).astype(F32).astype(BF16)
    count = packed.shape[1] // lanes
    tail = iota((height - count * block, rows), 0)
    tail = jnp.where(tail < cap, tail, -(10**6))
    for d in range(group):
        for n in range(count):
            send_ref[d, n * block : (n + 1) * block, :] = packed[
                d * block : (d + 1) * block, n * lanes : (n + 1) * lanes
            ]
        in_slot = (slot == (tail + (step * group + d) * cap).astype(F32)).astype(F32).astype(BF16)
        send_ref[d, count * block :, :] = lax.dot_general(
            in_slot, of_member, NT, preferred_element_type=F32
        ).astype(BF16)


def dispatch_kernel(cap, slot_ref, tokens_ref, out_ref, pieces, sem):
    step = pl.program_id(0)
    half = pieces.shape[1]
    group = out_ref.shape[0] // (CHUNKS * cap)

    @pl.when(step == 0)
    def _():
        copies = load_pieces(tokens_ref, pieces, sem, slot_ref.shape[1], 2 * half, half, half)
        start_all(copies)
        wait_all(copies)

    here = rows_of_slots(slot_ref[...], cap, step * group, group)
    out_ref[...] = jnp.dot(spread(here, cap), pieces[...], preferred_element_type=F32).astype(BF16)


def back_kernel(
    cap, got_ref, b_ref, a_ref, first_ref, second_ref, rank_ref, mask_ref, pieces, sem
):
    step = pl.program_id(0)
    ranks = b_ref.shape[0]
    group, height, width = got_ref.shape
    block = CHUNKS * cap
    half = pieces.shape[1] // 2
    count = half // width
    copies = load_pieces(a_ref, pieces, sem, ranks, 2 * half, 0, 2 * half)

    @pl.when(step == 0)
    def _():
        start_all(copies)

    tail = height - (count + 1) * block
    _, slot = piece_and_slot(iota((block, tail), 0), cap)
    pick_mask = (iota((block, tail), 1) == slot).astype(F32).astype(BF16)
    b_pieces = jnp.concatenate(
        [b_ref[:, k * width : (k + 1) * width] for k in range(CHUNKS)], axis=0
    )
    wide = lax.dot_general(
        join(got_ref, 0, group, block, count, 1), b_pieces, NT, preferred_element_type=F32
    )
    part = pick_piece(wide, cap, ranks)
    fold = same_slot(cap)
    ranks_of = []
    for d in range(group):
        at = slice(d * block, (d + 1) * block)
        full = jnp.dot(
            fold, part[at, :], precision=lax.Precision.HIGHEST, preferred_element_type=F32
        )
        mask = jnp.dot(
            pick_mask, got_ref[d, (count + 1) * block :, :], preferred_element_type=F32
        )
        ranks_of.append((full * mask).astype(BF16))
        mask_ref[at, :] = mask.astype(BF16)
    rank_rows = jnp.concatenate(ranks_of, axis=0)
    rank_ref[...] = rank_rows

    @pl.when(step == 0)
    def _():
        wait_all(copies)

    back = (
        adapter_scale * jnp.dot(spread(rank_rows, cap), pieces[...], preferred_element_type=F32)
    ).astype(BF16)
    first_ref[...] = back[:, 0:half]
    second_ref[:, 0:half] = back[:, half:]
    second_ref[:, half:] = jnp.zeros((second_ref.shape[0], second_ref.shape[1] - half), BF16)


def forth_kernel(
    cap, first_ref, second_ref, mask_ref, a_ref, b_ref, _, out_ref, rank_ref, pieces, sem
):
    step = pl.program_id(0)
    ranks = b_ref.shape[0]
    block = CHUNKS * cap
    width = out_ref.shape[1]
    half = pieces.shape[1] // 2
    group = first_ref.shape[0]

    @pl.when(step == 0)
    def _():
        copies = load_pieces(a_ref, pieces, sem, ranks, 2 * half, 0, 2 * half)
        start_all(copies)
        wait_all(copies)

    b_pieces = jnp.concatenate(
        [b_ref[:, k * width : (k + 1) * width] for k in range(CHUNKS)], axis=0
    )
    wide = lax.dot_general(
        join(first_ref, 0, group, block, 0, half // first_ref.shape[2]),
        pieces[:, 0:half],
        NT,
        preferred_element_type=F32,
    ) + lax.dot_general(second_ref[...], pieces[:, half:], NT, preferred_element_type=F32)
    part = pick_piece(wide, cap, ranks)
    fold = same_slot(cap)
    full = jnp.concatenate(
        [
            jnp.dot(
                fold,
                part[d * block : (d + 1) * block, :],
                precision=lax.Precision.HIGHEST,
                preferred_element_type=F32,
            )
            for d in range(group)
        ],
        axis=0,
    )
    rank_rows = (full * mask_ref[...].astype(F32)).astype(BF16)
    rank_ref[...] = rank_rows
    out_ref[...] = (
        adapter_scale * jnp.dot(spread(rank_rows, cap), b_pieces, preferred_element_type=F32)
    ).astype(BF16)


def page_grad_kernel(cap, first_ref, second_ref, low_ref, rank_ref, ga_ref, gb_ref):
    ranks = rank_ref.shape[1]
    half = second_ref.shape[1]
    devices, _, narrow = first_ref.shape
    block = CHUNKS * cap
    count = half // narrow
    tokens = join(first_ref, 0, devices, block, 0, count)
    grads = join(first_ref, 0, devices, block, count, 1)
    rank_rows = spread(rank_ref[...], cap)
    left = lax.dot_general(rank_rows, tokens, TN, preferred_element_type=F32)
    right = lax.dot_general(rank_rows, second_ref[...], TN, preferred_element_type=F32)
    low = lax.dot_general(
        spread(low_ref[...], cap), grads, TN, preferred_element_type=F32
    )
    for k in range(CHUNKS):
        at, col = slice(k * ranks, (k + 1) * ranks), 2 * k * half
        ga_ref[:, col : col + half] = (adapter_scale * left[at, :]).astype(BF16)
        ga_ref[:, col + half : col + 2 * half] = (adapter_scale * right[at, :]).astype(BF16)
        gb_ref[:, k * narrow : (k + 1) * narrow] = (adapter_scale * low[at, :]).astype(BF16)


def pair_kernel(other_ref, tokens_ref, grads_ref, out_ref, sem):
    rows, narrow = grads_ref.shape
    half = (out_ref.shape[1] - narrow) // CHUNKS
    at = pl.multiple_of(other_ref[0] * half, half)
    copies = [
        pltpu.make_async_copy(
            tokens_ref.at[:, pl.ds(2 * k * half + at, half)],
            out_ref.at[:, pl.ds(k * half, half)],
            sem.at[k],
        )
        for k in range(CHUNKS)
    ]
    copies.append(
        pltpu.make_async_copy(
            grads_ref, out_ref.at[:, pl.ds(CHUNKS * half, narrow)], sem.at[CHUNKS]
        )
    )
    start_all(copies)
    wait_all(copies)


def pair_base_kernel(at_ref, tok_ref, grad_ref, pair_ref, *refs):
    weights, (out_ref, back_ref, theirs_ref) = refs[:-3], refs[-3:]
    rows, narrow = grad_ref.shape
    half_width = back_ref.shape[1]
    grads = jnp.concatenate([grad_ref[...], pair_ref[:, half_width:]], axis=0)
    total = jnp.zeros((2 * rows, narrow), F32)
    for n, ref in enumerate(weights):
        weight = ref[...]
        share = weight.shape[0]
        full = pl.multiple_of(at_ref[2 * n] * share, share)
        part = pl.multiple_of(at_ref[2 * n + 1] * share, share)
        toks = jnp.concatenate(
            [tok_ref[:, pl.ds(full, share)], pair_ref[:, pl.ds(part, share)]], axis=0
        )
        total = total + jnp.dot(toks, weight, preferred_element_type=F32)
        back = lax.dot_general(grads, weight, NT, preferred_element_type=F32)
        back_ref[:, pl.ds(part, share)] = back[0:rows, :]
        theirs_ref[:, pl.ds(part, share)] = back[rows:, :]
    out_ref[...] = total[0:rows, :]
    theirs_ref[:, half_width:] = total[rows:, :]


def base_kernel(tok_ref, grad_ref, w_ref, out_ref, back_ref):
    @pl.when(pl.program_id(0) == 0)
    def _():
        out_ref[...] = jnp.zeros_like(out_ref)

    weight = w_ref[...]
    out_ref[...] += jnp.dot(tok_ref[...], weight, preferred_element_type=F32)
    back_ref[...] = lax.dot_general(grad_ref[...], weight, NT, preferred_element_type=F32)


def combine_kernel(cap, half, which_ref, col_ref, got_ref, mine_ref, pair_ref, *refs):
    out_hbm, out, sem, base, base_sem = refs[-5:]
    devices, block, width = got_ref.shape
    cols = out.shape[2]
    stride = mine_ref.shape[1] // (CHUNKS * cols)
    offset = half if stride == 2 else 0
    rows = col_ref.shape[0]

    def load(ref):
        copies = [
            pltpu.make_async_copy(
                ref.at[:, pl.ds((stride * k + offset) * cols, cols)], base.at[k], base_sem.at[k]
            )
            for k in range(CHUNKS)
        ]
        start_all(copies)

    @pl.when(which_ref[0] == half)
    def _():
        load(mine_ref)

    @pl.when(which_ref[0] != half)
    def _():
        load(pair_ref)

    col = col_ref[:, 0:1]
    copies = []
    for k in range(CHUNKS):
        low = k * cap // 16 * 16
        high = min(-(-(k + 1) * cap // 16) * 16, block)
        count = high - low
        lane = iota((1, devices * count), 1)
        row = jnp.zeros_like(lane)
        for d in range(1, devices):
            row = row + (lane >= d * count).astype(jnp.int32)
        slot = lane - row * count + (low - k * cap)
        key = jnp.where((slot >= 0) & (slot < cap), row * cap + slot, -1).astype(F32)
        here = (col == key).astype(F32).astype(BF16)
        packed = jnp.concatenate([got_ref[d, low:high, :] for d in range(devices)], axis=0)
        back = jnp.dot(here, packed, preferred_element_type=F32)
        pltpu.make_async_copy(
            mine_ref.at[:, pl.ds(0, cols)], base.at[k], base_sem.at[k]
        ).wait()
        out[k] = (base[k] + back[:, 0:cols]).astype(BF16)
        copy = pltpu.make_async_copy(
            out.at[k], out_hbm.at[:, pl.ds((2 * k + half) * cols, cols)], sem.at[k]
        )
        copy.start()
        copies.append(copy)
        if half == 1:
            base_out_ref, projected_ref = refs[0], refs[2]
            at = slice(k * (width - cols), (k + 1) * (width - cols))
            projected_ref[:, at] = (base_out_ref[:, at] + back[:, cols:]).astype(BF16)
    wait_all(copies)


def call(kernel, deps=(), **options):
    deps = tuple(deps)
    specs = list(options.pop("in_specs"))
    count = len(specs)

    def body(*refs):
        kernel(*refs[:count], *refs[count + len(deps) :])

    run = pl.pallas_call(
        body, in_specs=specs + [pl.BlockSpec(memory_space=pl.ANY)] * len(deps), **options
    )
    return lambda *args: run(*args, *deps)


def held(x, deps):
    deps = tuple(deps)
    if not deps:
        return x
    any_spec = pl.BlockSpec(memory_space=pl.ANY)
    return call(
        lambda x_ref, out_ref: None,
        deps=deps,
        out_shape=in_hbm(x.shape, x.dtype),
        in_specs=[any_spec],
        out_specs=any_spec,
        input_output_aliases={0: 0},
        cost_estimate=cost(0, 0),
        name="held",
    )(x)


def pick_kernel(count, which_ref, *refs):
    for n in range(count):

        @pl.when(which_ref[0] == n)
        def _():
            refs[count][...] = refs[n][...]


def pick(which, *arrays):
    x = arrays[0]
    return call(
        functools.partial(pick_kernel, len(arrays)),
        out_shape=jax.ShapeDtypeStruct(x.shape, x.dtype),
        in_specs=[pl.BlockSpec(memory_space=pltpu.SMEM)]
        + [pl.BlockSpec(memory_space=pltpu.VMEM)] * len(arrays),
        out_specs=pl.BlockSpec(memory_space=pltpu.VMEM),
        cost_estimate=cost(0, 2 * x.size * x.dtype.itemsize),
        name="pick",
    )(which.astype(jnp.int32).reshape(1), *arrays)


def in_hbm(shape, dtype):
    return pltpu.HBM(shape, dtype)


def whole(shape):
    return pl.BlockSpec(shape, lambda *_: (0,) * len(shape))


def params(semantics=None):
    return pltpu.CompilerParams(vmem_limit_bytes=VMEM_LIMIT, dimension_semantics=semantics)


def cost(flops, nbytes):
    return pl.CostEstimate(flops=int(flops), bytes_accessed=int(nbytes), transcendentals=0)


def swap(x, axis):
    size = lax.axis_size(axis)
    return lax.ppermute(x, axis, [(i, i ^ 1) for i in range(size)])


def gather_shares(base_weight, inner):
    count = lax.axis_size("fsdp")
    z = lax.axis_index("fsdp") // inner
    share = base_weight.shape[0] // 4
    at = lax.axis_index("tenant") * 2 + lax.axis_index("groups")
    mine = lax.dynamic_slice_in_dim(base_weight, at * share, share, 0)

    up_pairs = [(i, i + inner) for i in range(count - inner)]
    up, down = [mine], [mine]
    for j in range(1, 4):
        moved = [p for p in up_pairs if p[0] // inner >= j - 1]
        up.append(lax.ppermute(up[-1], "fsdp", moved))
        moved = [(b, a) for a, b in up_pairs if b // inner <= 4 - j]
        down.append(lax.ppermute(down[-1], "fsdp", moved))

    def of_z(*values):
        return functools.reduce(
            lambda rest, k: jnp.where(z == k, values[k], rest), range(3), values[3]
        )

    held_shares = [
        (mine, z),
        (pick(of_z(0, 1, 1, 1), down[1], up[1]), of_z(1, 0, 1, 2)),
        (pick(of_z(0, 1, 1, 2), down[2], down[1], up[2]), of_z(2, 2, 3, 1)),
        (pick(of_z(0, 1, 2, 3), down[3], down[2], up[2], up[3]), of_z(3, 3, 0, 0)),
    ]
    blocks, y_of, x_of, both_of = [], [], [], []

    def spread_share(n, deps=()):
        own, place = held_shares[n]
        y_of.append(held(swap(own, "fsdp"), deps))
        x_of.append(swap(own, "groups"))
        both_of.append(swap(y_of[n], "groups"))
        blocks.extend(
            [
                (own, place, 0, 0),
                (y_of[n], place, 1, 0),
                (x_of[n], place, 0, 1),
                (both_of[n], place, 1, 1),
            ]
        )

    for n in range(3):
        spread_share(n)
    after = {
        "first": [up[1], down[1]],
        "second": [up[2], down[2], y_of[0], x_of[0], y_of[1], x_of[1]],
        "third": [up[3], down[3], y_of[2], x_of[2], both_of[0], both_of[1]],
    }

    def last(deps):
        spread_share(3, deps)
        return [y_of[3], x_of[3], both_of[2]]

    return {"blocks": blocks, "after": after, "last": last}


def for_pair(tokens, grad_out):
    rows, width = tokens.shape
    narrow = grad_out.shape[1]
    any_spec = pl.BlockSpec(memory_space=pl.ANY)
    other = (1 - lax.axis_index("tenant")).astype(jnp.int32).reshape(1)
    return call(
        pair_kernel,
        out_shape=in_hbm((rows, width // 2 + narrow), BF16),
        in_specs=[pl.BlockSpec(memory_space=pltpu.SMEM), any_spec, any_spec],
        out_specs=any_spec,
        scratch_shapes=[pltpu.SemaphoreType.DMA((CHUNKS + 1,))],
        compiler_params=params(),
        cost_estimate=cost(0, 4 * rows * (width // 2 + narrow)),
        name="for_pair",
    )(other, tokens, grad_out)


def paired_base(tokens, grad_out, pair, shares, fsdp_size, inner):
    rows, width = tokens.shape
    narrow = grad_out.shape[1]
    tenant, group = lax.axis_index("tenant"), lax.axis_index("groups")
    fsdp = lax.axis_index("fsdp")
    y = fsdp % inner
    gathered = shares["blocks"]
    any_spec = pl.BlockSpec(memory_space=pl.ANY)
    vmem = pl.BlockSpec(memory_space=pltpu.VMEM)
    smem = pl.BlockSpec(memory_space=pltpu.SMEM)

    half = width // 2
    at = []
    for _, place, dy, dx in gathered:
        shard = place * inner + (y ^ dy)
        x = group ^ dx
        at += [shard * 4 + tenant * 2 + x, shard * 2 + x]
    out, back, theirs = call(
        pair_base_kernel,
        out_shape=(
            jax.ShapeDtypeStruct((rows, narrow), F32),
            jax.ShapeDtypeStruct((rows, half), F32),
            jax.ShapeDtypeStruct((rows, half + narrow), F32),
        ),
        in_specs=[smem] + [vmem] * (3 + len(gathered)),
        out_specs=(vmem, vmem, vmem),
        compiler_params=params(),
        cost_estimate=cost(4 * rows * width * narrow, width * narrow),
        name="base",
    )(jnp.stack(at).astype(jnp.int32), tokens, grad_out, pair, *[g[0] for g in gathered])
    theirs = swap(theirs, "tenant")
    return out + theirs[:, half:], back, theirs


def whole_base(tokens, grad_out, base_weight):
    rows, width = tokens.shape
    narrow = grad_out.shape[1]
    wp = width // CHUNKS
    group_size, tenant_size = lax.axis_size("groups"), lax.axis_size("tenant")
    shares = group_size * tenant_size
    share = base_weight.shape[0] // shares
    which = lax.axis_index("groups") * tenant_size + lax.axis_index("tenant")
    mine = lax.dynamic_slice_in_dim(base_weight, which * share, share, 0)
    weight = lax.all_gather(mine, ("fsdp", "groups", "tenant"), axis=0, tiled=True)
    return call(
        base_kernel,
        out_shape=(
            jax.ShapeDtypeStruct((rows, narrow), F32),
            jax.ShapeDtypeStruct((rows, width), F32),
        ),
        grid=(CHUNKS,),
        in_specs=[
            pl.BlockSpec((rows, wp), lambda i: (0, i)),
            whole((rows, narrow)),
            pl.BlockSpec((wp, narrow), lambda i: (i, 0)),
        ],
        out_specs=(whole((rows, narrow)), pl.BlockSpec((rows, wp), lambda i: (0, i))),
        compiler_params=params(("arbitrary",)),
        cost_estimate=cost(4 * rows * width * narrow, 2 * width * narrow),
        name="base",
    )(tokens, grad_out, weight)


def on_device(tokens, grad_out, base_weight, page_a, page_b, page_owner, row_tenant):
    rows, width = tokens.shape
    narrow = grad_out.shape[1]
    fsdp_size = lax.axis_size("fsdp")
    tenant_size = lax.axis_size("tenant")
    devices = fsdp_size * tenant_size
    cap = max(4, 4 * rows // (3 * devices))
    per_page = page_a.shape[1] // RANK
    ranks = page_a.shape[1]
    block = CHUNKS * cap
    total = devices * block
    wp, np_ = width // CHUNKS, narrow // CHUNKS
    half = wp // 2
    height = (half // np_ + 1) * block + -(-cap // 16) * 16
    left_factor, right_factor = page_a[0], page_b[0]
    axes = ("fsdp", "tenant")
    which = lax.axis_index("tenant").astype(jnp.int32).reshape(1)

    def exchange(x):
        return lax.all_to_all(x, axes, split_axis=0, concat_axis=0, tiled=True)

    any_spec = pl.BlockSpec(memory_space=pl.ANY)
    smem = pl.BlockSpec(memory_space=pltpu.SMEM)
    paired = (
        fsdp_size == 8
        and tenant_size == 2
        and lax.axis_size("groups") == 2
        and width // fsdp_size == wp
    )

    steps = 4 if devices % 4 == 0 else 1
    send_first, slot_row, slot_col = call(
        functools.partial(route_kernel, devices, cap, per_page),
        out_shape=(
            in_hbm((devices, height, np_), BF16),
            jax.ShapeDtypeStruct((1, rows), F32),
            jax.ShapeDtypeStruct((rows, rows), F32),
        ),
        grid=(steps,),
        in_specs=[smem, whole((1, rows)), any_spec, any_spec],
        out_specs=(
            pl.BlockSpec((devices // steps, height, np_), lambda i: (i, 0, 0)),
            whole((1, rows)),
            whole((rows, rows)),
        ),
        scratch_shapes=[
            pltpu.VMEM((CHUNKS * rows, half + np_), BF16),
            pltpu.SemaphoreType.DMA((2 * CHUNKS,)),
        ],
        compiler_params=params(("arbitrary",)),
        cost_estimate=cost(total * rows * width, 2 * total * half),
        name="route",
    )(page_owner, row_tenant.reshape(1, rows), tokens, grad_out)
    after = {}
    if paired:
        shares = gather_shares(base_weight, 2)
        after = shares["after"]
    part = total // steps
    send_second = call(
        functools.partial(dispatch_kernel, cap),
        out_shape=in_hbm((total, half), BF16),
        grid=(steps,),
        in_specs=[whole((1, rows)), any_spec],
        out_specs=pl.BlockSpec((part, half), lambda i: (i, 0)),
        scratch_shapes=[
            pltpu.VMEM((CHUNKS * rows, half), BF16),
            pltpu.SemaphoreType.DMA((CHUNKS,)),
        ],
        compiler_params=params(("arbitrary",)),
        cost_estimate=cost(total * rows * width, 2 * total * half),
        name="dispatch",
    )(slot_row, tokens)
    if paired:
        pair = for_pair(tokens, grad_out)
    got_first = exchange(held(send_first, after.get("first", ())))
    got_second = exchange(held(send_second, [got_first] + after.get("second", [])))

    back_first, back_second, rank_rows, mask_rows = call(
        functools.partial(back_kernel, cap),
        out_shape=(
            in_hbm((total, half), BF16),
            in_hbm((total, half + np_), BF16),
            jax.ShapeDtypeStruct((total, ranks), BF16),
            jax.ShapeDtypeStruct((total, ranks), BF16),
        ),
        grid=(steps,),
        in_specs=[
            pl.BlockSpec((devices // steps, height, np_), lambda i: (i, 0, 0)),
            whole((ranks, narrow)),
            any_spec,
        ],
        out_specs=(
            pl.BlockSpec((part, half), lambda i: (i, 0)),
            pl.BlockSpec((part, half + np_), lambda i: (i, 0)),
            pl.BlockSpec((part, ranks), lambda i: (i, 0)),
            pl.BlockSpec((part, ranks), lambda i: (i, 0)),
        ),
        scratch_shapes=[
            pltpu.VMEM((CHUNKS * ranks, wp), BF16),
            pltpu.SemaphoreType.DMA((CHUNKS,)),
        ],
        compiler_params=params(("arbitrary",)),
        cost_estimate=cost(2 * total * ranks * width, 2 * (total * wp + ranks * width)),
        name="rank_grad_back",
    )(got_first, right_factor, left_factor)
    got_back = exchange(held(back_first, [got_second] + after.get("third", [])))

    back_second, low_rows = call(
        functools.partial(forth_kernel, cap),
        out_shape=(
            in_hbm((total, half + np_), BF16),
            jax.ShapeDtypeStruct((total, ranks), BF16),
        ),
        grid=(steps,),
        in_specs=[
            pl.BlockSpec((devices // steps, height, np_), lambda i: (i, 0, 0)),
            pl.BlockSpec((part, half), lambda i: (i, 0)),
            pl.BlockSpec((part, ranks), lambda i: (i, 0)),
            any_spec,
            whole((ranks, narrow)),
            any_spec,
        ],
        out_specs=(
            pl.BlockSpec((part, np_), lambda i: (i, half // np_)),
            pl.BlockSpec((part, ranks), lambda i: (i, 0)),
        ),
        scratch_shapes=[
            pltpu.VMEM((CHUNKS * ranks, wp), BF16),
            pltpu.SemaphoreType.DMA((CHUNKS,)),
        ],
        input_output_aliases={5: 0},
        compiler_params=params(("arbitrary",)),
        cost_estimate=cost(2 * total * ranks * width, 2 * (total * wp + ranks * width)),
        name="lowrank_out",
    )(got_first, got_second, mask_rows, left_factor, right_factor, back_second)
    fourth = shares["last"]([low_rows]) if paired else []
    got_rest = exchange(held(back_second, [got_back] + fourth))

    if paired:
        base_out, base_mine, base_pair = paired_base(
            tokens, grad_out, held(swap(pair, "tenant"), [low_rows]), shares, fsdp_size, 2
        )
    else:
        base_out, base_mine = whole_base(tokens, grad_out, base_weight)
        base_pair = base_mine

    grad_a, grad_b = call(
        functools.partial(page_grad_kernel, cap),
        in_specs=[pl.BlockSpec(memory_space=pltpu.VMEM)] * 4,
        out_shape=(
            jax.ShapeDtypeStruct((ranks, width), BF16),
            jax.ShapeDtypeStruct((ranks, narrow), BF16),
        ),
        compiler_params=params(),
        cost_estimate=cost(2 * total * ranks * width, 2 * (total * wp + ranks * width)),
        name="page_grads",
    )(got_first, got_second, low_rows, rank_rows)

    combine_cost = cost(rows * total * width, 2 * total * half + 4 * rows * width)
    combine_scratch = [
        pltpu.VMEM((CHUNKS, rows, half), BF16),
        pltpu.SemaphoreType.DMA((CHUNKS,)),
        pltpu.VMEM((CHUNKS, rows, half), F32),
        pltpu.SemaphoreType.DMA((CHUNKS,)),
    ]
    vmem = pl.BlockSpec(memory_space=pltpu.VMEM)
    grad_tokens = call(
        functools.partial(combine_kernel, cap, 0),
        out_shape=jax.ShapeDtypeStruct((rows, width), BF16),
        in_specs=[smem, vmem, vmem, any_spec, any_spec],
        out_specs=any_spec,
        scratch_shapes=combine_scratch,
        compiler_params=params(),
        cost_estimate=combine_cost,
        name="combine_first",
    )(which, slot_col, got_back.reshape(devices, block, half), base_mine, base_pair)
    projected, grad_tokens = call(
        functools.partial(combine_kernel, cap, 1),
        out_shape=(
            jax.ShapeDtypeStruct((rows, narrow), BF16),
            jax.ShapeDtypeStruct((rows, width), BF16),
        ),
        in_specs=[smem, vmem, vmem, any_spec, any_spec, vmem, any_spec],
        out_specs=(vmem, any_spec),
        scratch_shapes=combine_scratch,
        input_output_aliases={6: 1},
        compiler_params=params(),
        cost_estimate=combine_cost,
        name="combine_rest",
    )(
        which,
        slot_col,
        got_rest.reshape(devices, block, half + np_),
        base_mine,
        base_pair,
        base_out,
        grad_tokens,
    )

    return projected, grad_tokens, grad_a[None], grad_b[None]


def solution(mesh):
    rows = P(("groups", "fsdp", "tenant"), None)
    pages = P(("groups", "fsdp", "tenant"), None, None)
    return jax.shard_map(
        on_device,
        mesh=mesh,
        in_specs=(
            rows,
            rows,
            P("fsdp", None),
            pages,
            pages,
            P("groups"),
            P(("groups", "fsdp", "tenant")),
        ),
        out_specs=(rows, rows, pages, pages),
        check_vma=False,
    )
```

```python
import functools

import jax
import jax.numpy as jnp
from jax import lax
from jax.experimental import pallas as pl
from jax.experimental.pallas import tpu as pltpu
from jax.sharding import PartitionSpec as P

RANK = 32
CHUNKS = 8
FIRST = 4
VMEM_LIMIT = 60 * 1024 * 1024

adapter_scale = 2.0

F32 = jnp.float32
BF16 = jnp.bfloat16
NT = (((1,), (1,)), ((), ()))
TN = (((0,), (0,)), ((), ()))


def iota(shape, dim):
    return lax.broadcasted_iota(jnp.int32, shape, dim)


def piece_and_slot(index, cap):
    piece = jnp.zeros_like(index)
    for k in range(1, CHUNKS + 1):
        piece = piece + (index >= k * cap).astype(jnp.int32)
    return piece, index - piece * cap


def spread_mask(rows, cap, lanes):
    block = CHUNKS * cap
    piece, _ = piece_and_slot(iota((block, CHUNKS * lanes), 0), cap)
    group = jnp.zeros_like(piece)
    lane = iota(piece.shape, 1)
    for k in range(1, CHUNKS):
        group = group + (lane >= k * lanes).astype(jnp.int32)
    mask = (piece == group).astype(F32).astype(BF16)
    return jnp.concatenate([mask] * (rows // block), axis=0)


def spread(rows, cap):
    return jnp.concatenate([rows] * CHUNKS, axis=1) * spread_mask(
        rows.shape[0], cap, rows.shape[1]
    )


def pick_piece(wide, cap, lanes):
    block, n = CHUNKS * cap, wide.shape[0]
    piece, _ = piece_and_slot(iota((block, lanes), 0), cap)
    piece = jnp.concatenate([piece] * (n // block), axis=0)
    total = jnp.zeros((n, lanes), F32)
    for k in range(CHUNKS):
        total = total + jnp.where(piece == k, wide[:, k * lanes : (k + 1) * lanes], 0.0)
    return total


def same_slot(cap):
    shape = (CHUNKS * cap, CHUNKS * cap)
    _, slot = piece_and_slot(iota(shape, 0), cap)
    _, slot_c = piece_and_slot(iota(shape, 1), cap)
    return (slot == slot_c).astype(F32)


def fold_pieces(fold, part):
    terms, left = [], part
    for _ in range(3):
        terms.append(left.astype(BF16))
        left = left - terms[-1].astype(F32)
    wide = jnp.dot(
        fold.astype(BF16), jnp.concatenate(terms, axis=1), preferred_element_type=F32
    )
    n = part.shape[1]
    return wide[:, 0:n] + (wide[:, n : 2 * n] + wide[:, 2 * n :])


def load_pieces(src, dst, sem, height, stride, start, width):
    return [
        pltpu.make_async_copy(
            src.at[:, pl.ds(k * stride + start, width)],
            dst.at[pl.ds(k * height, height), pl.ds(0, width)],
            sem.at[k],
        )
        for k in range(CHUNKS)
    ]


def start_all(copies):
    for copy in copies:
        copy.start()


def wait_all(copies):
    for copy in copies:
        copy.wait()


def rows_of_slots(slot, cap, first, group):
    _, slot_of = piece_and_slot(iota((CHUNKS * cap, slot.shape[1]), 0), cap)
    return jnp.concatenate(
        [
            (slot == (slot_of + (first + d) * cap).astype(F32)).astype(F32).astype(BF16)
            for d in range(group)
        ],
        axis=0,
    )


def earlier_rows(rows):
    return (iota((rows, rows), 0) < iota((rows, rows), 1)).astype(F32).astype(BF16)


def grad_pieces(ref, block):
    return jnp.concatenate([ref[d, 0:block, :] for d in range(ref.shape[0])], axis=0)


def route_kernel(
    devices, cap, per_page, owner_ref, tenant_ref, grads_ref, send_ref, row_ref, col_ref
):
    rows = tenant_ref.shape[1]
    height, lanes = send_ref.shape[1:]
    block = CHUNKS * cap
    page = tenant_ref[...] // per_page
    member = tenant_ref[...] - page * per_page

    def add_page(p, target):
        return target + jnp.where(page == p, owner_ref[p], 0)

    target = lax.fori_loop(0, owner_ref.shape[0], add_page, jnp.zeros_like(page))
    chosen = (iota((devices, rows), 0) == target).astype(F32)
    before = jnp.dot(chosen.astype(BF16), earlier_rows(rows), preferred_element_type=F32)
    slot = target.astype(F32) * cap + jnp.sum(before * chosen, axis=0, keepdims=True)
    row_ref[...] = slot
    col_ref[...] = jnp.transpose(jnp.broadcast_to(slot, (rows, rows)))

    pieces = jnp.concatenate(
        [grads_ref[:, k * lanes : (k + 1) * lanes] for k in range(CHUNKS)], axis=0
    )
    here = spread(rows_of_slots(slot, cap, 0, devices), cap)
    packed = jnp.dot(here, pieces, preferred_element_type=F32).astype(BF16)
    of_member = (iota((lanes, rows), 0) // RANK == member).astype(F32).astype(BF16)
    tail = iota((height - block, rows), 0)
    tail = jnp.where(tail < cap, tail, -(10**6))
    in_slot = jnp.concatenate(
        [(slot == (tail + d * cap).astype(F32)).astype(F32).astype(BF16) for d in range(devices)],
        axis=0,
    )
    masks = lax.dot_general(in_slot, of_member, NT, preferred_element_type=F32).astype(BF16)
    extra = height - block
    for d in range(devices):
        send_ref[d, 0:block, :] = packed[d * block : (d + 1) * block, :]
        send_ref[d, block:, :] = masks[d * extra : (d + 1) * extra, :]


def dispatch_kernel(cap, slot_ref, tokens_ref, out_ref, pieces, sem):
    step = pl.program_id(0)
    rows, width = slot_ref.shape[1], pieces.shape[1]
    group = out_ref.shape[0] // (CHUNKS * cap)

    @pl.when(step == 0)
    def _():
        copies = load_pieces(tokens_ref, pieces, sem, rows, width, 0, width)
        start_all(copies)
        wait_all(copies)

    here = rows_of_slots(slot_ref[...], cap, step * group, group)
    out_ref[...] = jnp.dot(spread(here, cap), pieces[...], preferred_element_type=F32).astype(BF16)


def back_kernel(
    cap, got_ref, b_ref, a_ref, first_ref, second_ref, rank_ref, mask_ref, pieces, sem
):
    step = pl.program_id(0)
    ranks = b_ref.shape[0]
    group, height, width = got_ref.shape
    block = CHUNKS * cap
    split = first_ref.shape[1]
    rest = pieces.shape[1] - split
    copies = load_pieces(a_ref, pieces, sem, ranks, split + rest, 0, split + rest)

    @pl.when(step == 0)
    def _():
        start_all(copies)

    tail = height - block
    _, slot = piece_and_slot(iota((block, tail), 0), cap)
    pick_mask = (iota((block, tail), 1) == slot).astype(F32).astype(BF16)
    b_pieces = jnp.concatenate(
        [b_ref[:, k * width : (k + 1) * width] for k in range(CHUNKS)], axis=0
    )
    wide = lax.dot_general(
        grad_pieces(got_ref, block), b_pieces, NT, preferred_element_type=F32
    )
    part = pick_piece(wide, cap, ranks)
    fold = same_slot(cap)
    ranks_of = []
    for d in range(group):
        at = slice(d * block, (d + 1) * block)
        full = fold_pieces(fold, part[at, :])
        mask = jnp.dot(pick_mask, got_ref[d, block:, :], preferred_element_type=F32)
        ranks_of.append((full * mask).astype(BF16))
        mask_ref[at, :] = mask.astype(BF16)
    rank_rows = jnp.concatenate(ranks_of, axis=0)
    rank_ref[...] = rank_rows

    @pl.when(step == 0)
    def _():
        wait_all(copies)

    back = (
        adapter_scale * jnp.dot(spread(rank_rows, cap), pieces[...], preferred_element_type=F32)
    ).astype(BF16)
    first_ref[...] = back[:, 0:split]
    second_ref[:, 0:rest] = back[:, split:]
    second_ref[:, rest:] = jnp.zeros((second_ref.shape[0], second_ref.shape[1] - rest), BF16)


def forth_kernel(
    cap, tok_ref, mask_ref, a_ref, b_ref, _, out_ref, rank_ref, pieces, sem
):
    step = pl.program_id(0)
    ranks = b_ref.shape[0]
    block = CHUNKS * cap
    width = out_ref.shape[1]
    wide_piece = pieces.shape[1]
    group = tok_ref.shape[0] // block

    @pl.when(step == 0)
    def _():
        copies = load_pieces(a_ref, pieces, sem, ranks, wide_piece, 0, wide_piece)
        start_all(copies)
        wait_all(copies)

    b_pieces = jnp.concatenate(
        [b_ref[:, k * width : (k + 1) * width] for k in range(CHUNKS)], axis=0
    )
    wide = lax.dot_general(tok_ref[...], pieces[...], NT, preferred_element_type=F32)
    part = pick_piece(wide, cap, ranks)
    fold = same_slot(cap)
    full = jnp.concatenate(
        [
            fold_pieces(fold, part[d * block : (d + 1) * block, :])
            for d in range(group)
        ],
        axis=0,
    )
    rank_rows = (full * mask_ref[...].astype(F32)).astype(BF16)
    rank_ref[...] = rank_rows
    out_ref[...] = (
        adapter_scale * jnp.dot(spread(rank_rows, cap), b_pieces, preferred_element_type=F32)
    ).astype(BF16)


def page_grad_kernel(cap, tok_ref, grad_ref, low_ref, rank_ref, ga_ref, gb_ref):
    ranks = rank_ref.shape[1]
    wide, narrow = tok_ref.shape[1], grad_ref.shape[2]
    left = lax.dot_general(
        spread(rank_ref[...], cap), tok_ref[...], TN, preferred_element_type=F32
    )
    grads = grad_pieces(grad_ref, CHUNKS * cap)
    right = lax.dot_general(spread(low_ref[...], cap), grads, TN, preferred_element_type=F32)
    for k in range(CHUNKS):
        at = slice(k * ranks, (k + 1) * ranks)
        ga_ref[:, k * wide : (k + 1) * wide] = (adapter_scale * left[at, :]).astype(BF16)
        gb_ref[:, k * narrow : (k + 1) * narrow] = (adapter_scale * right[at, :]).astype(BF16)


def pair_kernel(other_ref, tokens_ref, grads_ref, out_ref, sem):
    rows, narrow = grads_ref.shape
    half = (out_ref.shape[1] - narrow) // CHUNKS
    at = pl.multiple_of(other_ref[0] * half, half)
    copies = [
        pltpu.make_async_copy(
            tokens_ref.at[:, pl.ds(2 * k * half + at, half)],
            out_ref.at[:, pl.ds(k * half, half)],
            sem.at[k],
        )
        for k in range(CHUNKS)
    ]
    copies.append(
        pltpu.make_async_copy(
            grads_ref, out_ref.at[:, pl.ds(CHUNKS * half, narrow)], sem.at[CHUNKS]
        )
    )
    start_all(copies)
    wait_all(copies)


def pair_base_kernel(at_ref, tok_ref, grad_ref, pair_ref, *refs):
    weights, (out_ref, back_ref, theirs_ref) = refs[:-3], refs[-3:]
    rows, narrow = grad_ref.shape
    half_width = back_ref.shape[1]
    grads = jnp.concatenate([grad_ref[...], pair_ref[:, half_width:]], axis=0)
    total = jnp.zeros((2 * rows, narrow), F32)
    share = 2 * half_width // at_ref.shape[0]
    parts = [ref.at[pl.ds(r, share), :] for ref in weights for r in range(0, ref.shape[0], share)]
    for n, ref in enumerate(parts):
        weight = ref[...]
        full = pl.multiple_of(at_ref[2 * n] * share, share)
        part = pl.multiple_of(at_ref[2 * n + 1] * share, share)
        toks = jnp.concatenate(
            [tok_ref[:, pl.ds(full, share)], pair_ref[:, pl.ds(part, share)]], axis=0
        )
        total = total + jnp.dot(toks, weight, preferred_element_type=F32)
        back = lax.dot_general(grads, weight, NT, preferred_element_type=F32)
        back_ref[:, pl.ds(part, share)] = back[0:rows, :]
        theirs_ref[:, pl.ds(part, share)] = back[rows:, :]
    out_ref[...] = total[0:rows, :]
    theirs_ref[:, half_width:] = total[rows:, :]


def base_kernel(tok_ref, grad_ref, w_ref, out_ref, back_ref):
    @pl.when(pl.program_id(0) == 0)
    def _():
        out_ref[...] = jnp.zeros_like(out_ref)

    weight = w_ref[...]
    out_ref[...] += jnp.dot(tok_ref[...], weight, preferred_element_type=F32)
    back_ref[...] = lax.dot_general(grad_ref[...], weight, NT, preferred_element_type=F32)


def combine_kernel(cap, start, which_ref, col_ref, got_ref, mine_ref, pair_ref, *refs):
    out_hbm, out, sem, base, base_sem = refs[-5:]
    devices, block, width = got_ref.shape
    cols = out.shape[2]
    rows = col_ref.shape[0]
    piece = out_hbm.shape[1] // CHUNKS
    parts = 2 if mine_ref.shape[1] < out_hbm.shape[1] else 1
    size = piece // parts

    def load(ref, part):
        low, high = max(start, part * size), min(start + cols, (part + 1) * size)
        if low < high:
            start_all(
                [
                    pltpu.make_async_copy(
                        ref.at[:, pl.ds(k * size + low - part * size, high - low)],
                        base.at[k, :, pl.ds(low - start, high - low)],
                        base_sem.at[k],
                    )
                    for k in range(CHUNKS)
                ]
            )

    if parts == 1:
        load(mine_ref, 0)
    else:
        for n in range(2):

            @pl.when(which_ref[0] == n)
            def _():
                load(mine_ref, n)
                load(pair_ref, 1 - n)

    col = col_ref[:, 0:1]
    copies = []
    for k in range(CHUNKS):
        low = k * cap // 16 * 16
        high = min(-(-(k + 1) * cap // 16) * 16, block)
        count = high - low
        lane = iota((1, devices * count), 1)
        row = jnp.zeros_like(lane)
        for d in range(1, devices):
            row = row + (lane >= d * count).astype(jnp.int32)
        slot = lane - row * count + (low - k * cap)
        key = jnp.where((slot >= 0) & (slot < cap), row * cap + slot, -1).astype(F32)
        here = (col == key).astype(F32).astype(BF16)
        packed = jnp.concatenate([got_ref[d, low:high, :] for d in range(devices)], axis=0)
        back = jnp.dot(here, packed, preferred_element_type=F32)
        pltpu.make_async_copy(base.at[k], base.at[k], base_sem.at[k]).wait()
        out[k] = (base[k] + back[:, 0:cols]).astype(BF16)
        copy = pltpu.make_async_copy(
            out.at[k], out_hbm.at[:, pl.ds(k * piece + start, cols)], sem.at[k]
        )
        copy.start()
        copies.append(copy)
        if width > cols:
            outs, projected_ref = refs[: len(refs) - 7], refs[-6]
            at = slice(k * (width - cols), (k + 1) * (width - cols))
            total = sum(ref[:, at] for ref in outs)
            projected_ref[:, at] = (total + back[:, cols:]).astype(BF16)
    wait_all(copies)


def call(kernel, deps=(), **options):
    specs = list(options.pop("in_specs"))
    count, extra = len(specs), len(deps)

    def body(*refs):
        kernel(*refs[:count], *refs[count + extra :])

    run = pl.pallas_call(
        body, in_specs=specs + [pl.BlockSpec(memory_space=pl.ANY)] * extra, **options
    )
    return lambda *args: run(*args, *deps)


def hbm(*arrays):
    kept = tuple(pltpu.with_memory_space_constraint(x, pltpu.HBM) for x in arrays)
    return kept if len(kept) > 1 else kept[0]


def held(x, deps):
    deps = tuple(deps)
    if not deps:
        return x
    any_spec = pl.BlockSpec(memory_space=pl.ANY)
    return call(
        lambda x_ref, out_ref: None,
        deps=deps,
        out_shape=in_hbm(x.shape, x.dtype),
        in_specs=[any_spec],
        out_specs=any_spec,
        input_output_aliases={0: 0},
        compiler_params=params(),
        cost_estimate=cost(0, 0),
        name="held",
    )(x)


def pick_kernel(count, which_ref, *refs):
    for n in range(count):

        @pl.when(which_ref[0] == n)
        def _():
            refs[count][...] = refs[n][...]


def pick(which, *arrays):
    x = arrays[0]
    return call(
        functools.partial(pick_kernel, len(arrays)),
        out_shape=in_hbm(x.shape, x.dtype),
        in_specs=[pl.BlockSpec(memory_space=pltpu.SMEM)]
        + [pl.BlockSpec(memory_space=pltpu.VMEM)] * len(arrays),
        out_specs=pl.BlockSpec(memory_space=pltpu.VMEM),
        compiler_params=params(),
        cost_estimate=cost(0, 2 * x.size * x.dtype.itemsize),
        name="pick",
    )(which.astype(jnp.int32).reshape(1), *arrays)


def in_hbm(shape, dtype):
    return pltpu.HBM(shape, dtype)


def whole(shape):
    return pl.BlockSpec(shape, lambda *_: (0,) * len(shape))


def params(semantics=None):
    return pltpu.CompilerParams(vmem_limit_bytes=VMEM_LIMIT, dimension_semantics=semantics)


def cost(flops, nbytes):
    return pl.CostEstimate(flops=1, bytes_accessed=1, transcendentals=0)


def swap(x, axis):
    size = lax.axis_size(axis)
    return lax.ppermute(x, axis, [(i, i ^ 1) for i in range(size)])


def gather_shares(base_weight, inner):
    count = lax.axis_size("fsdp")
    z = lax.axis_index("fsdp") // inner
    share = base_weight.shape[0] // 4
    at = lax.axis_index("tenant") * 2 + lax.axis_index("groups")
    mine = lax.dynamic_slice_in_dim(base_weight, at * share, share, 0)

    up_pairs = [(i, i + inner) for i in range(count - inner)]
    up, down = [mine], [mine]
    for j in range(1, 4):
        moved = [p for p in up_pairs if p[0] // inner >= j - 1]
        up.append(lax.ppermute(up[-1], "fsdp", moved))
        moved = [(b, a) for a, b in up_pairs if b // inner <= 4 - j]
        down.append(lax.ppermute(down[-1], "fsdp", moved))

    def of_z(*values):
        return functools.reduce(
            lambda rest, k: jnp.where(z == k, values[k], rest), range(3), values[3]
        )

    held_shares = [
        (mine, [z]),
        (pick(of_z(0, 1, 1, 1), down[1], up[1]), [of_z(1, 0, 1, 2)]),
        (pick(of_z(0, 1, 1, 2), down[2], down[1], up[2]), [of_z(2, 2, 3, 1)]),
        (pick(of_z(0, 1, 2, 3), down[3], down[2], up[2], up[3]), [of_z(3, 3, 0, 0)]),
    ]
    blocks, y_of, x_of, both_of = [], [], [], []

    def spread_share(n, deps=()):
        own, place = held_shares[n]
        y_of.append(held(swap(own, "fsdp"), deps))
        x_of.append(swap(own, "groups"))
        both_of.append(swap(y_of[n], "groups"))
        blocks.extend(
            [
                (own, place, 0, 0),
                (y_of[n], place, 1, 0),
                (x_of[n], place, 0, 1),
                (both_of[n], place, 1, 1),
            ]
        )

    for n in range(3):
        spread_share(n)
    after = {
        "first": [up[2], down[2], y_of[0], x_of[0]],
        "third": [up[3], down[3], y_of[1], x_of[1], both_of[0], y_of[2], x_of[2], both_of[1]],
    }

    def last(deps):
        spread_share(3, deps)
        return [y_of[3], x_of[3]]

    return {"blocks": blocks, "after": after, "last": last}


def for_pair(tokens, grad_out):
    rows, width = tokens.shape
    narrow = grad_out.shape[1]
    any_spec = pl.BlockSpec(memory_space=pl.ANY)
    other = (1 - lax.axis_index("tenant")).astype(jnp.int32).reshape(1)
    return call(
        pair_kernel,
        out_shape=in_hbm((rows, width // 2 + narrow), BF16),
        in_specs=[pl.BlockSpec(memory_space=pltpu.SMEM), any_spec, any_spec],
        out_specs=pl.BlockSpec(memory_space=pltpu.VMEM),
        scratch_shapes=[pltpu.SemaphoreType.DMA((CHUNKS + 1,))],
        compiler_params=params(),
        cost_estimate=cost(0, 4 * rows * (width // 2 + narrow)),
        name="for_pair",
    )(other, tokens, grad_out)


def paired_base(tokens, grad_out, pair, shares, fsdp_size, inner):
    rows, width = tokens.shape
    narrow = grad_out.shape[1]
    tenant, group = lax.axis_index("tenant"), lax.axis_index("groups")
    fsdp = lax.axis_index("fsdp")
    y = fsdp % inner
    gathered = shares["blocks"]
    any_spec = pl.BlockSpec(memory_space=pl.ANY)
    vmem = pl.BlockSpec(memory_space=pltpu.VMEM)
    smem = pl.BlockSpec(memory_space=pltpu.SMEM)

    half = width // 2
    at = []
    for _, places, dy, dx in gathered:
        for place in places:
            shard = place * inner + (y ^ dy)
            x = group ^ dx
            at += [shard * 4 + tenant * 2 + x, shard * 2 + x]
    out, back, theirs = call(
        pair_base_kernel,
        out_shape=(
            in_hbm((rows, narrow), F32),
            in_hbm((rows, half), F32),
            in_hbm((rows, half + narrow), F32),
        ),
        in_specs=[smem] + [vmem] * (3 + len(gathered)),
        out_specs=(vmem, vmem, vmem),
        compiler_params=params(),
        cost_estimate=cost(4 * rows * width * narrow, width * narrow),
        name="base",
    )(jnp.stack(at).astype(jnp.int32), tokens, grad_out, pair, *[g[0] for g in gathered])
    theirs = swap(theirs, "tenant")
    return hbm(out), hbm(back), hbm(theirs)


def whole_base(tokens, grad_out, base_weight):
    rows, width = tokens.shape
    narrow = grad_out.shape[1]
    wp = width // CHUNKS
    group_size, tenant_size = lax.axis_size("groups"), lax.axis_size("tenant")
    shares = group_size * tenant_size
    share = base_weight.shape[0] // shares
    which = lax.axis_index("groups") * tenant_size + lax.axis_index("tenant")
    mine = lax.dynamic_slice_in_dim(base_weight, which * share, share, 0)
    weight = lax.all_gather(mine, ("fsdp", "groups", "tenant"), axis=0, tiled=True)
    return call(
        base_kernel,
        out_shape=(
            in_hbm((rows, narrow), F32),
            in_hbm((rows, width), F32),
        ),
        grid=(CHUNKS,),
        in_specs=[
            pl.BlockSpec((rows, wp), lambda i: (0, i)),
            whole((rows, narrow)),
            pl.BlockSpec((wp, narrow), lambda i: (i, 0)),
        ],
        out_specs=(whole((rows, narrow)), pl.BlockSpec((rows, wp), lambda i: (0, i))),
        compiler_params=params(("arbitrary",)),
        cost_estimate=cost(4 * rows * width * narrow, 2 * width * narrow),
        name="base",
    )(tokens, grad_out, weight)


def on_device(tokens, grad_out, base_weight, page_a, page_b, page_owner, row_tenant):
    rows, width = tokens.shape
    narrow = grad_out.shape[1]
    fsdp_size = lax.axis_size("fsdp")
    tenant_size = lax.axis_size("tenant")
    devices = fsdp_size * tenant_size
    cap = max(4, 4 * rows // (3 * devices))
    per_page = page_a.shape[1] // RANK
    ranks = page_a.shape[1]
    block = CHUNKS * cap
    total = devices * block
    wp, np_ = width // CHUNKS, narrow // CHUNKS
    split = wp // 128 * FIRST // 8 * 128
    rest = wp - split
    height = block + -(-cap // 16) * 16
    left_factor, right_factor = hbm(page_a[0], page_b[0])
    tokens, grad_out = hbm(tokens, grad_out)
    axes = ("fsdp", "tenant")
    which = lax.axis_index("tenant").astype(jnp.int32).reshape(1)

    def exchange(x):
        return lax.all_to_all(x, axes, split_axis=0, concat_axis=0, tiled=True)

    any_spec = pl.BlockSpec(memory_space=pl.ANY)
    smem = pl.BlockSpec(memory_space=pltpu.SMEM)
    paired = (
        fsdp_size == 8
        and tenant_size == 2
        and lax.axis_size("groups") == 2
        and width // fsdp_size == wp
    )

    steps = 4 if devices % 4 == 0 else 1
    send_grads, slot_row, slot_col = call(
        functools.partial(route_kernel, devices, cap, per_page),
        out_shape=(
            in_hbm((devices, height, np_), BF16),
            in_hbm((1, rows), F32),
            in_hbm((rows, rows), F32),
        ),
        in_specs=[smem] + [pl.BlockSpec(memory_space=pltpu.VMEM)] * 2,
        out_specs=tuple(pl.BlockSpec(memory_space=pltpu.VMEM) for _ in range(3)),
        compiler_params=params(),
        cost_estimate=cost(2 * total * rows * narrow, 4 * total * np_),
        name="route",
    )(page_owner, row_tenant.reshape(1, rows), grad_out)
    slot_row, slot_col = hbm(slot_row, slot_col)
    got_grads = exchange(send_grads)

    steps = 4 if devices % 4 == 0 else 1
    part = total // steps
    send_tokens = call(
        functools.partial(dispatch_kernel, cap),
        out_shape=in_hbm((total, wp), BF16),
        grid=(steps,),
        in_specs=[whole((1, rows)), any_spec],
        out_specs=pl.BlockSpec((part, wp), lambda i: (i, 0)),
        scratch_shapes=[
            pltpu.VMEM((CHUNKS * rows, wp), BF16),
            pltpu.SemaphoreType.DMA((CHUNKS,)),
        ],
        compiler_params=params(("arbitrary",)),
        cost_estimate=cost(2 * total * rows * width, 4 * total * wp),
        name="dispatch",
    )(slot_row, tokens)
    after = {}
    if paired:
        shares = gather_shares(base_weight, 2)
        after = shares["after"]
        pair = swap(for_pair(tokens, grad_out), "tenant")
        after["third"].append(pair)
    got_tokens = exchange(held(send_tokens, [got_grads] + after.get("first", [])))

    back_first, back_second, rank_rows, mask_rows = call(
        functools.partial(back_kernel, cap),
        out_shape=(
            in_hbm((total, split), BF16),
            in_hbm((total, rest + np_), BF16),
            in_hbm((total, ranks), BF16),
            in_hbm((total, ranks), BF16),
        ),
        grid=(steps,),
        in_specs=[
            pl.BlockSpec((devices // steps, height, np_), lambda i: (i, 0, 0)),
            whole((ranks, narrow)),
            any_spec,
        ],
        out_specs=(
            pl.BlockSpec((part, split), lambda i: (i, 0)),
            pl.BlockSpec((part, rest + np_), lambda i: (i, 0)),
            pl.BlockSpec((part, ranks), lambda i: (i, 0)),
            pl.BlockSpec((part, ranks), lambda i: (i, 0)),
        ),
        scratch_shapes=[
            pltpu.VMEM((CHUNKS * ranks, wp), BF16),
            pltpu.SemaphoreType.DMA((CHUNKS,)),
        ],
        compiler_params=params(("arbitrary",)),
        cost_estimate=cost(2 * total * ranks * width, 2 * (total * wp + ranks * width)),
        name="rank_grad_back",
    )(got_grads, right_factor, left_factor)
    rank_rows, mask_rows = hbm(rank_rows, mask_rows)
    got_back = exchange(held(back_first, [got_tokens] + after.get("third", [])))

    back_second, low_rows = call(
        functools.partial(forth_kernel, cap),
        out_shape=(
            in_hbm((total, rest + np_), BF16),
            in_hbm((total, ranks), BF16),
        ),
        grid=(steps,),
        in_specs=[
            pl.BlockSpec((part, wp), lambda i: (i, 0)),
            pl.BlockSpec((part, ranks), lambda i: (i, 0)),
            any_spec,
            whole((ranks, narrow)),
            any_spec,
        ],
        out_specs=(
            pl.BlockSpec((part, np_), lambda i: (i, rest // np_)),
            pl.BlockSpec((part, ranks), lambda i: (i, 0)),
        ),
        scratch_shapes=[
            pltpu.VMEM((CHUNKS * ranks, wp), BF16),
            pltpu.SemaphoreType.DMA((CHUNKS,)),
        ],
        input_output_aliases={4: 0},
        compiler_params=params(("arbitrary",)),
        cost_estimate=cost(2 * total * ranks * width, 2 * (total * wp + ranks * width)),
        name="lowrank_out",
    )(got_tokens, mask_rows, left_factor, right_factor, hbm(back_second))
    low_rows = hbm(low_rows)
    fourth = shares["last"]([low_rows]) if paired else []
    got_rest = exchange(held(back_second, [got_back] + fourth))

    if paired:
        base_out, base_mine, base_pair = paired_base(
            tokens, grad_out, held(pair, [low_rows]), shares, fsdp_size, 2
        )
    else:
        base_out, base_mine = whole_base(tokens, grad_out, base_weight)
        base_pair = base_mine
    outs, out_specs = [base_out], [whole((rows, narrow))]
    if paired:
        outs.append(base_pair)
        out_specs.append(pl.BlockSpec((rows, narrow), lambda i: (0, width // 2 // narrow)))

    grad_a, grad_b = call(
        functools.partial(page_grad_kernel, cap),
        in_specs=[pl.BlockSpec(memory_space=pltpu.VMEM)] * 4,
        out_shape=(
            in_hbm((ranks, width), BF16),
            in_hbm((ranks, narrow), BF16),
        ),
        compiler_params=params(),
        cost_estimate=cost(2 * total * ranks * width, 2 * (total * wp + ranks * width)),
        name="page_grads",
    )(got_tokens, got_grads, low_rows, rank_rows)

    combine_cost = cost(rows * total * width, total * wp + 4 * rows * width)

    def combine_scratch(cols):
        return [
            pltpu.VMEM((CHUNKS, rows, cols), BF16),
            pltpu.SemaphoreType.DMA((CHUNKS,)),
            pltpu.VMEM((CHUNKS, rows, cols), F32),
            pltpu.SemaphoreType.DMA((CHUNKS,)),
        ]

    grad_tokens = call(
        functools.partial(combine_kernel, cap, 0),
        out_shape=in_hbm((rows, width), BF16),
        grid=(1,),
        in_specs=[smem, whole((rows, rows)), whole((devices, block, split)), any_spec, any_spec],
        out_specs=any_spec,
        scratch_shapes=combine_scratch(split),
        compiler_params=params(),
        cost_estimate=combine_cost,
        name="combine_first",
    )(which, slot_col, got_back.reshape(devices, block, split), base_mine, base_pair)
    projected, grad_tokens = call(
        functools.partial(combine_kernel, cap, split),
        out_shape=(
            in_hbm((rows, narrow), BF16),
            in_hbm((rows, width), BF16),
        ),
        grid=(1,),
        in_specs=[smem, whole((rows, rows)), whole((devices, block, rest + np_)), any_spec, any_spec, *out_specs, any_spec],
        out_specs=(whole((rows, narrow)), any_spec),
        scratch_shapes=combine_scratch(rest),
        input_output_aliases={5 + len(out_specs): 1},
        compiler_params=params(),
        cost_estimate=combine_cost,
        name="combine_rest",
    )(
        which,
        slot_col,
        got_rest.reshape(devices, block, rest + np_),
        base_mine,
        base_pair,
        *outs,
        grad_tokens,
    )

    return projected, grad_tokens, grad_a[None], grad_b[None]


def solution(mesh):
    rows = P(("groups", "fsdp", "tenant"), None)
    pages = P(("groups", "fsdp", "tenant"), None, None)
    return jax.shard_map(
        on_device,
        mesh=mesh,
        in_specs=(
            rows,
            rows,
            P("fsdp", None),
            pages,
            pages,
            P("groups"),
            P(("groups", "fsdp", "tenant")),
        ),
        out_specs=(rows, rows, pages, pages),
        check_vma=False,
    )
```

```python
import functools

import jax
import jax.numpy as jnp
from jax import lax
from jax.experimental import pallas as pl
from jax.experimental.pallas import tpu as pltpu
from jax.sharding import PartitionSpec as P

RANK = 32
CHUNKS = 8
FIRST = 4
VMEM_LIMIT = 60 * 1024 * 1024

adapter_scale = 2.0

F32 = jnp.float32
BF16 = jnp.bfloat16
NT = (((1,), (1,)), ((), ()))
TN = (((0,), (0,)), ((), ()))


def iota(shape, dim):
    return lax.broadcasted_iota(jnp.int32, shape, dim)


def piece_and_slot(index, cap):
    piece = jnp.zeros_like(index)
    for k in range(1, CHUNKS + 1):
        piece = piece + (index >= k * cap).astype(jnp.int32)
    return piece, index - piece * cap


def spread_mask(rows, cap, lanes):
    block = CHUNKS * cap
    piece, _ = piece_and_slot(iota((block, CHUNKS * lanes), 0), cap)
    group = jnp.zeros_like(piece)
    lane = iota(piece.shape, 1)
    for k in range(1, CHUNKS):
        group = group + (lane >= k * lanes).astype(jnp.int32)
    mask = (piece == group).astype(F32).astype(BF16)
    return jnp.concatenate([mask] * (rows // block), axis=0)


def spread(rows, cap):
    return jnp.concatenate([rows] * CHUNKS, axis=1) * spread_mask(
        rows.shape[0], cap, rows.shape[1]
    )


def pick_piece(wide, cap, lanes):
    block, n = CHUNKS * cap, wide.shape[0]
    piece, _ = piece_and_slot(iota((block, lanes), 0), cap)
    piece = jnp.concatenate([piece] * (n // block), axis=0)
    total = jnp.zeros((n, lanes), F32)
    for k in range(CHUNKS):
        total = total + jnp.where(piece == k, wide[:, k * lanes : (k + 1) * lanes], 0.0)
    return total


def same_slot(cap):
    shape = (CHUNKS * cap, CHUNKS * cap)
    _, slot = piece_and_slot(iota(shape, 0), cap)
    _, slot_c = piece_and_slot(iota(shape, 1), cap)
    return (slot == slot_c).astype(F32)


def fold_pieces(fold, part):
    terms, left = [], part
    for _ in range(3):
        terms.append(left.astype(BF16))
        left = left - terms[-1].astype(F32)
    wide = jnp.dot(
        fold.astype(BF16), jnp.concatenate(terms, axis=1), preferred_element_type=F32
    )
    n = part.shape[1]
    return wide[:, 0:n] + (wide[:, n : 2 * n] + wide[:, 2 * n :])


def load_pieces(src, dst, sem, height, stride, start, width):
    return [
        pltpu.make_async_copy(
            src.at[:, pl.ds(k * stride + start, width)],
            dst.at[pl.ds(k * height, height), pl.ds(0, width)],
            sem.at[k],
        )
        for k in range(CHUNKS)
    ]


def start_all(copies):
    for copy in copies:
        copy.start()


def wait_all(copies):
    for copy in copies:
        copy.wait()


def rows_of_slots(slot, cap, first, group):
    _, slot_of = piece_and_slot(iota((CHUNKS * cap, slot.shape[1]), 0), cap)
    return jnp.concatenate(
        [
            (slot == (slot_of + (first + d) * cap).astype(F32)).astype(F32).astype(BF16)
            for d in range(group)
        ],
        axis=0,
    )


def earlier_rows(rows):
    return (iota((rows, rows), 0) < iota((rows, rows), 1)).astype(F32).astype(BF16)


def grad_pieces(ref, block):
    return jnp.concatenate([ref[d, 0:block, :] for d in range(ref.shape[0])], axis=0)


def route_kernel(
    devices, cap, per_page, owner_ref, tenant_ref, grads_ref, send_ref, row_ref, col_ref
):
    rows = tenant_ref.shape[1]
    height, lanes = send_ref.shape[1:]
    block = CHUNKS * cap
    page = tenant_ref[...] // per_page
    member = tenant_ref[...] - page * per_page

    def add_page(p, target):
        return target + jnp.where(page == p, owner_ref[p], 0)

    target = lax.fori_loop(0, owner_ref.shape[0], add_page, jnp.zeros_like(page))
    chosen = (iota((devices, rows), 0) == target).astype(F32)
    before = jnp.dot(chosen.astype(BF16), earlier_rows(rows), preferred_element_type=F32)
    slot = target.astype(F32) * cap + jnp.sum(before * chosen, axis=0, keepdims=True)
    row_ref[...] = slot
    col_ref[...] = jnp.transpose(jnp.broadcast_to(slot, (rows, rows)))

    pieces = jnp.concatenate(
        [grads_ref[:, k * lanes : (k + 1) * lanes] for k in range(CHUNKS)], axis=0
    )
    here = spread(rows_of_slots(slot, cap, 0, devices), cap)
    packed = jnp.dot(here, pieces, preferred_element_type=F32).astype(BF16)
    of_member = (iota((lanes, rows), 0) // RANK == member).astype(F32).astype(BF16)
    tail = iota((height - block, rows), 0)
    tail = jnp.where(tail < cap, tail, -(10**6))
    in_slot = jnp.concatenate(
        [(slot == (tail + d * cap).astype(F32)).astype(F32).astype(BF16) for d in range(devices)],
        axis=0,
    )
    masks = lax.dot_general(in_slot, of_member, NT, preferred_element_type=F32).astype(BF16)
    extra = height - block
    for d in range(devices):
        send_ref[d, 0:block, :] = packed[d * block : (d + 1) * block, :]
        send_ref[d, block:, :] = masks[d * extra : (d + 1) * extra, :]


def dispatch_kernel(cap, slot_ref, tokens_ref, out_ref, pieces, sem):
    step = pl.program_id(0)
    rows, width = slot_ref.shape[1], pieces.shape[1]
    group = out_ref.shape[0] // (CHUNKS * cap)

    @pl.when(step == 0)
    def _():
        copies = load_pieces(tokens_ref, pieces, sem, rows, width, 0, width)
        start_all(copies)
        wait_all(copies)

    here = rows_of_slots(slot_ref[...], cap, step * group, group)
    out_ref[...] = jnp.dot(spread(here, cap), pieces[...], preferred_element_type=F32).astype(BF16)


def back_kernel(
    cap, got_ref, b_ref, a_ref, first_ref, second_ref, rank_ref, mask_ref, pieces, sem
):
    step = pl.program_id(0)
    ranks = b_ref.shape[0]
    group, height, width = got_ref.shape
    block = CHUNKS * cap
    split = first_ref.shape[1]
    rest = pieces.shape[1] - split
    copies = load_pieces(a_ref, pieces, sem, ranks, split + rest, 0, split + rest)

    @pl.when(step == 0)
    def _():
        start_all(copies)

    tail = height - block
    _, slot = piece_and_slot(iota((block, tail), 0), cap)
    pick_mask = (iota((block, tail), 1) == slot).astype(F32).astype(BF16)
    b_pieces = jnp.concatenate(
        [b_ref[:, k * width : (k + 1) * width] for k in range(CHUNKS)], axis=0
    )
    wide = lax.dot_general(
        grad_pieces(got_ref, block), b_pieces, NT, preferred_element_type=F32
    )
    part = pick_piece(wide, cap, ranks)
    fold = same_slot(cap)
    ranks_of = []
    for d in range(group):
        at = slice(d * block, (d + 1) * block)
        full = fold_pieces(fold, part[at, :])
        mask = jnp.dot(pick_mask, got_ref[d, block:, :], preferred_element_type=F32)
        ranks_of.append((full * mask).astype(BF16))
        mask_ref[at, :] = mask.astype(BF16)
    rank_rows = jnp.concatenate(ranks_of, axis=0)
    rank_ref[...] = rank_rows

    @pl.when(step == 0)
    def _():
        wait_all(copies)

    back = (
        adapter_scale * jnp.dot(spread(rank_rows, cap), pieces[...], preferred_element_type=F32)
    ).astype(BF16)
    first_ref[...] = back[:, 0:split]
    second_ref[:, 0:rest] = back[:, split:]
    second_ref[:, rest:] = jnp.zeros((second_ref.shape[0], second_ref.shape[1] - rest), BF16)


def forth_kernel(
    cap, tok_ref, mask_ref, a_ref, b_ref, _, out_ref, rank_ref, pieces, sem
):
    step = pl.program_id(0)
    ranks = b_ref.shape[0]
    block = CHUNKS * cap
    width = out_ref.shape[1]
    wide_piece = pieces.shape[1]
    group = tok_ref.shape[0] // block

    @pl.when(step == 0)
    def _():
        copies = load_pieces(a_ref, pieces, sem, ranks, wide_piece, 0, wide_piece)
        start_all(copies)
        wait_all(copies)

    b_pieces = jnp.concatenate(
        [b_ref[:, k * width : (k + 1) * width] for k in range(CHUNKS)], axis=0
    )
    wide = lax.dot_general(tok_ref[...], pieces[...], NT, preferred_element_type=F32)
    part = pick_piece(wide, cap, ranks)
    fold = same_slot(cap)
    full = jnp.concatenate(
        [
            fold_pieces(fold, part[d * block : (d + 1) * block, :])
            for d in range(group)
        ],
        axis=0,
    )
    rank_rows = (full * mask_ref[...].astype(F32)).astype(BF16)
    rank_ref[...] = rank_rows
    out_ref[...] = (
        adapter_scale * jnp.dot(spread(rank_rows, cap), b_pieces, preferred_element_type=F32)
    ).astype(BF16)


def page_grad_kernel(cap, tok_ref, grad_ref, low_ref, rank_ref, ga_ref, gb_ref):
    ranks = rank_ref.shape[1]
    wide, narrow = tok_ref.shape[1], grad_ref.shape[2]
    left = lax.dot_general(
        spread(rank_ref[...], cap), tok_ref[...], TN, preferred_element_type=F32
    )
    grads = grad_pieces(grad_ref, CHUNKS * cap)
    right = lax.dot_general(spread(low_ref[...], cap), grads, TN, preferred_element_type=F32)
    for k in range(CHUNKS):
        at = slice(k * ranks, (k + 1) * ranks)
        ga_ref[:, k * wide : (k + 1) * wide] = (adapter_scale * left[at, :]).astype(BF16)
        gb_ref[:, k * narrow : (k + 1) * narrow] = (adapter_scale * right[at, :]).astype(BF16)


def pair_kernel(other_ref, tokens_ref, grads_ref, out_ref, sem):
    rows, narrow = grads_ref.shape
    half = (out_ref.shape[1] - narrow) // CHUNKS
    at = pl.multiple_of(other_ref[0] * half, half)
    copies = [
        pltpu.make_async_copy(
            tokens_ref.at[:, pl.ds(2 * k * half + at, half)],
            out_ref.at[:, pl.ds(k * half, half)],
            sem.at[k],
        )
        for k in range(CHUNKS)
    ]
    copies.append(
        pltpu.make_async_copy(
            grads_ref, out_ref.at[:, pl.ds(CHUNKS * half, narrow)], sem.at[CHUNKS]
        )
    )
    start_all(copies)
    wait_all(copies)


def pair_base_kernel(at_ref, tok_ref, grad_ref, pair_ref, *refs):
    weights, (out_ref, back_ref, theirs_ref) = refs[:-3], refs[-3:]
    rows, narrow = grad_ref.shape
    half_width = back_ref.shape[1]
    grads = jnp.concatenate([grad_ref[...], pair_ref[:, half_width:]], axis=0)
    total = jnp.zeros((2 * rows, narrow), F32)
    share = 2 * half_width // at_ref.shape[0]
    parts = [ref.at[pl.ds(r, share), :] for ref in weights for r in range(0, ref.shape[0], share)]
    for n, ref in enumerate(parts):
        weight = ref[...]
        full = pl.multiple_of(at_ref[2 * n] * share, share)
        part = pl.multiple_of(at_ref[2 * n + 1] * share, share)
        toks = jnp.concatenate(
            [tok_ref[:, pl.ds(full, share)], pair_ref[:, pl.ds(part, share)]], axis=0
        )
        total = total + jnp.dot(toks, weight, preferred_element_type=F32)
        back = lax.dot_general(grads, weight, NT, preferred_element_type=F32)
        back_ref[:, pl.ds(part, share)] = back[0:rows, :]
        theirs_ref[:, pl.ds(part, share)] = back[rows:, :]
    out_ref[...] = total[0:rows, :]
    theirs_ref[:, half_width:] = total[rows:, :]


def base_kernel(tok_ref, grad_ref, w_ref, out_ref, back_ref):
    @pl.when(pl.program_id(0) == 0)
    def _():
        out_ref[...] = jnp.zeros_like(out_ref)

    weight = w_ref[...]
    out_ref[...] += jnp.dot(tok_ref[...], weight, preferred_element_type=F32)
    back_ref[...] = lax.dot_general(grad_ref[...], weight, NT, preferred_element_type=F32)


def combine_kernel(cap, start, extra, which_ref, col_hbm, got_hbm, mine_ref, pair_ref, *refs):
    extras, refs = refs[:extra], refs[extra:]
    if extra:
        projected_ref, refs = refs[1], refs[2:]
    out_hbm, out, sem, base, base_sem, got_ref, col_ref, in_sem, *sums = refs
    devices, block, width = got_ref.shape
    cols = out.shape[2]
    piece = out_hbm.shape[1] // CHUNKS
    parts = 2 if mine_ref.shape[1] < out_hbm.shape[1] else 1
    size = piece // parts
    group = devices // 4 if devices % 4 == 0 else devices

    loads = [pltpu.make_async_copy(col_hbm, col_ref, in_sem.at[0])]
    for n in range(devices // group):
        at = pl.ds(n * group, group)
        loads.append(pltpu.make_async_copy(got_hbm.at[at], got_ref.at[at], in_sem.at[1 + n]))
    late = []
    for n, ref in enumerate(sums):
        last = pl.ds(extras[n].shape[1] - ref.shape[1], ref.shape[1])
        late.append(pltpu.make_async_copy(extras[n].at[:, last], ref, in_sem.at[5 + n]))

    def load(ref, part):
        low, high = max(start, part * size), min(start + cols, (part + 1) * size)
        if low < high:
            start_all(
                [
                    pltpu.make_async_copy(
                        ref.at[:, pl.ds(k * size + low - part * size, high - low)],
                        base.at[k, :, pl.ds(low - start, high - low)],
                        base_sem.at[k],
                    )
                    for k in range(CHUNKS)
                ]
            )

    start_all(loads)
    if parts == 1:
        load(mine_ref, 0)
    else:
        for n in range(2):

            @pl.when(which_ref[0] == n)
            def _():
                load(mine_ref, n)
                load(pair_ref, 1 - n)

    start_all(late)
    wait_all(loads)
    col, rows = col_ref[:, 0:1], col_ref.shape[0]
    copies = []
    for k in range(0, CHUNKS, 2):
        low = k * cap // 16 * 16
        high = min(-(-(k + 2) * cap // 16) * 16, block)
        count = high - low
        lane = iota((1, devices * count), 1)
        row = jnp.zeros_like(lane)
        for d in range(1, devices):
            row = row + (lane >= d * count).astype(jnp.int32)
        slot = lane - row * count + low
        here = []
        for n in (k, k + 1):
            mine = (slot >= n * cap) & (slot < (n + 1) * cap)
            key = jnp.where(mine, row * cap + slot - n * cap, -1).astype(F32)
            here.append((col == key).astype(F32).astype(BF16))
        packed = jnp.concatenate([got_ref[d, low:high, :] for d in range(devices)], axis=0)
        both = jnp.dot(jnp.concatenate(here, axis=0), packed, preferred_element_type=F32)
        for n in (k, k + 1):
            back = both[(n - k) * rows : (n - k + 1) * rows, :]
            pltpu.make_async_copy(base.at[n], base.at[n], base_sem.at[n]).wait()
            out[n] = (base[n] + back[:, 0:cols]).astype(BF16)
            copy = pltpu.make_async_copy(
                out.at[n], out_hbm.at[:, pl.ds(n * piece + start, cols)], sem.at[n]
            )
            copy.start()
            copies.append(copy)
            if extra:
                if n == 0:
                    wait_all(late)
                at = slice(n * (width - cols), (n + 1) * (width - cols))
                total = sum(ref[:, at] for ref in sums) + back[:, cols:]
                projected_ref[:, at] = total.astype(BF16)
    wait_all(copies)


def call(kernel, deps=(), **options):
    specs = list(options.pop("in_specs"))
    count, extra = len(specs), len(deps)

    def body(*refs):
        kernel(*refs[:count], *refs[count + extra :])

    run = pl.pallas_call(
        body, in_specs=specs + [pl.BlockSpec(memory_space=pl.ANY)] * extra, **options
    )
    return lambda *args: run(*args, *deps)


def hbm(*arrays):
    kept = tuple(pltpu.with_memory_space_constraint(x, pltpu.HBM) for x in arrays)
    return kept if len(kept) > 1 else kept[0]


def held(x, deps):
    deps = tuple(deps)
    if not deps:
        return x
    any_spec = pl.BlockSpec(memory_space=pl.ANY)
    return call(
        lambda x_ref, out_ref: None,
        deps=deps,
        out_shape=in_hbm(x.shape, x.dtype),
        in_specs=[any_spec],
        out_specs=any_spec,
        input_output_aliases={0: 0},
        compiler_params=params(),
        cost_estimate=cost(0, 0),
        name="held",
    )(x)


def pick_kernel(count, which_ref, *refs):
    for n in range(count):

        @pl.when(which_ref[0] == n)
        def _():
            refs[count][...] = refs[n][...]


def pick(which, *arrays):
    x = arrays[0]
    return call(
        functools.partial(pick_kernel, len(arrays)),
        out_shape=in_hbm(x.shape, x.dtype),
        in_specs=[pl.BlockSpec(memory_space=pltpu.SMEM)]
        + [pl.BlockSpec(memory_space=pltpu.VMEM)] * len(arrays),
        out_specs=pl.BlockSpec(memory_space=pltpu.VMEM),
        compiler_params=params(),
        cost_estimate=cost(0, 2 * x.size * x.dtype.itemsize),
        name="pick",
    )(which.astype(jnp.int32).reshape(1), *arrays)


def in_hbm(shape, dtype):
    return pltpu.HBM(shape, dtype)


def whole(shape):
    return pl.BlockSpec(shape, lambda *_: (0,) * len(shape))


def params(semantics=None):
    return pltpu.CompilerParams(vmem_limit_bytes=VMEM_LIMIT, dimension_semantics=semantics)


def cost(flops, nbytes):
    return pl.CostEstimate(flops=1, bytes_accessed=1, transcendentals=0)


def swap(x, axis):
    size = lax.axis_size(axis)
    return lax.ppermute(x, axis, [(i, i ^ 1) for i in range(size)])


def gather_shares(base_weight, inner):
    count = lax.axis_size("fsdp")
    z = lax.axis_index("fsdp") // inner
    share = base_weight.shape[0] // 4
    at = lax.axis_index("tenant") * 2 + lax.axis_index("groups")
    mine = lax.dynamic_slice_in_dim(base_weight, at * share, share, 0)

    up_pairs = [(i, i + inner) for i in range(count - inner)]
    up, down = [mine], [mine]
    for j in range(1, 4):
        moved = [p for p in up_pairs if p[0] // inner >= j - 1]
        up.append(lax.ppermute(up[-1], "fsdp", moved))
        moved = [(b, a) for a, b in up_pairs if b // inner <= 4 - j]
        down.append(lax.ppermute(down[-1], "fsdp", moved))

    def of_z(*values):
        return functools.reduce(
            lambda rest, k: jnp.where(z == k, values[k], rest), range(3), values[3]
        )

    held_shares = [
        (mine, [z]),
        (pick(of_z(0, 1, 1, 1), down[1], up[1]), [of_z(1, 0, 1, 2)]),
        (pick(of_z(0, 1, 1, 2), down[2], down[1], up[2]), [of_z(2, 2, 3, 1)]),
        (pick(of_z(0, 1, 2, 3), down[3], down[2], up[2], up[3]), [of_z(3, 3, 0, 0)]),
    ]
    blocks, y_of, x_of, both_of = [], [], [], []

    def spread_share(n, deps=()):
        own, place = held_shares[n]
        y_of.append(held(swap(own, "fsdp"), deps))
        x_of.append(swap(own, "groups"))
        both_of.append(swap(y_of[n], "groups"))
        blocks.extend(
            [
                (own, place, 0, 0),
                (y_of[n], place, 1, 0),
                (x_of[n], place, 0, 1),
                (both_of[n], place, 1, 1),
            ]
        )

    for n in range(3):
        spread_share(n)
    after = {
        "first": [up[2], down[2], y_of[0], x_of[0]],
        "third": [up[3], down[3], y_of[1], x_of[1], both_of[0], y_of[2], x_of[2], both_of[1]],
    }

    def last(deps):
        spread_share(3, deps)
        return [y_of[3], x_of[3]]

    return {"blocks": blocks, "after": after, "last": last}


def for_pair(tokens, grad_out):
    rows, width = tokens.shape
    narrow = grad_out.shape[1]
    any_spec = pl.BlockSpec(memory_space=pl.ANY)
    other = (1 - lax.axis_index("tenant")).astype(jnp.int32).reshape(1)
    return call(
        pair_kernel,
        out_shape=in_hbm((rows, width // 2 + narrow), BF16),
        in_specs=[pl.BlockSpec(memory_space=pltpu.SMEM), any_spec, any_spec],
        out_specs=pl.BlockSpec(memory_space=pltpu.VMEM),
        scratch_shapes=[pltpu.SemaphoreType.DMA((CHUNKS + 1,))],
        compiler_params=params(),
        cost_estimate=cost(0, 4 * rows * (width // 2 + narrow)),
        name="for_pair",
    )(other, tokens, grad_out)


def paired_base(tokens, grad_out, pair, shares, fsdp_size, inner):
    rows, width = tokens.shape
    narrow = grad_out.shape[1]
    tenant, group = lax.axis_index("tenant"), lax.axis_index("groups")
    fsdp = lax.axis_index("fsdp")
    y = fsdp % inner
    gathered = shares["blocks"]
    any_spec = pl.BlockSpec(memory_space=pl.ANY)
    vmem = pl.BlockSpec(memory_space=pltpu.VMEM)
    smem = pl.BlockSpec(memory_space=pltpu.SMEM)

    half = width // 2
    at = []
    for _, places, dy, dx in gathered:
        for place in places:
            shard = place * inner + (y ^ dy)
            x = group ^ dx
            at += [shard * 4 + tenant * 2 + x, shard * 2 + x]
    out, back, theirs = call(
        pair_base_kernel,
        out_shape=(
            in_hbm((rows, narrow), F32),
            in_hbm((rows, half), F32),
            in_hbm((rows, half + narrow), F32),
        ),
        in_specs=[smem] + [vmem] * (3 + len(gathered)),
        out_specs=(vmem, vmem, vmem),
        compiler_params=params(),
        cost_estimate=cost(4 * rows * width * narrow, width * narrow),
        name="base",
    )(jnp.stack(at).astype(jnp.int32), tokens, grad_out, pair, *[g[0] for g in gathered])
    theirs = swap(theirs, "tenant")
    return hbm(out), hbm(back), hbm(theirs)


def whole_base(tokens, grad_out, base_weight):
    rows, width = tokens.shape
    narrow = grad_out.shape[1]
    wp = width // CHUNKS
    group_size, tenant_size = lax.axis_size("groups"), lax.axis_size("tenant")
    shares = group_size * tenant_size
    share = base_weight.shape[0] // shares
    which = lax.axis_index("groups") * tenant_size + lax.axis_index("tenant")
    mine = lax.dynamic_slice_in_dim(base_weight, which * share, share, 0)
    weight = lax.all_gather(mine, ("fsdp", "groups", "tenant"), axis=0, tiled=True)
    return call(
        base_kernel,
        out_shape=(
            in_hbm((rows, narrow), F32),
            in_hbm((rows, width), F32),
        ),
        grid=(CHUNKS,),
        in_specs=[
            pl.BlockSpec((rows, wp), lambda i: (0, i)),
            whole((rows, narrow)),
            pl.BlockSpec((wp, narrow), lambda i: (i, 0)),
        ],
        out_specs=(whole((rows, narrow)), pl.BlockSpec((rows, wp), lambda i: (0, i))),
        compiler_params=params(("arbitrary",)),
        cost_estimate=cost(4 * rows * width * narrow, 2 * width * narrow),
        name="base",
    )(tokens, grad_out, weight)


def on_device(tokens, grad_out, base_weight, page_a, page_b, page_owner, row_tenant):
    rows, width = tokens.shape
    narrow = grad_out.shape[1]
    fsdp_size = lax.axis_size("fsdp")
    tenant_size = lax.axis_size("tenant")
    devices = fsdp_size * tenant_size
    cap = max(4, 4 * rows // (3 * devices))
    per_page = page_a.shape[1] // RANK
    ranks = page_a.shape[1]
    block = CHUNKS * cap
    total = devices * block
    wp, np_ = width // CHUNKS, narrow // CHUNKS
    split = wp // 128 * FIRST // 8 * 128
    rest = wp - split
    height = block + -(-cap // 16) * 16
    left_factor, right_factor = hbm(page_a[0], page_b[0])
    tokens, grad_out = hbm(tokens, grad_out)
    axes = ("fsdp", "tenant")
    which = lax.axis_index("tenant").astype(jnp.int32).reshape(1)

    def exchange(x):
        return lax.all_to_all(x, axes, split_axis=0, concat_axis=0, tiled=True)

    any_spec = pl.BlockSpec(memory_space=pl.ANY)
    smem = pl.BlockSpec(memory_space=pltpu.SMEM)
    paired = (
        fsdp_size == 8
        and tenant_size == 2
        and lax.axis_size("groups") == 2
        and width // fsdp_size == wp
    )

    steps = 4 if devices % 4 == 0 else 1
    send_grads, slot_row, slot_col = call(
        functools.partial(route_kernel, devices, cap, per_page),
        out_shape=(
            in_hbm((devices, height, np_), BF16),
            in_hbm((1, rows), F32),
            in_hbm((rows, rows), F32),
        ),
        in_specs=[smem] + [pl.BlockSpec(memory_space=pltpu.VMEM)] * 2,
        out_specs=tuple(pl.BlockSpec(memory_space=pltpu.VMEM) for _ in range(3)),
        compiler_params=params(),
        cost_estimate=cost(2 * total * rows * narrow, 4 * total * np_),
        name="route",
    )(page_owner, row_tenant.reshape(1, rows), grad_out)
    slot_row, slot_col = hbm(slot_row, slot_col)
    got_grads = exchange(send_grads)

    steps = 4 if devices % 4 == 0 else 1
    part = total // steps
    send_tokens = call(
        functools.partial(dispatch_kernel, cap),
        out_shape=in_hbm((total, wp), BF16),
        grid=(steps,),
        in_specs=[whole((1, rows)), any_spec],
        out_specs=pl.BlockSpec((part, wp), lambda i: (i, 0)),
        scratch_shapes=[
            pltpu.VMEM((CHUNKS * rows, wp), BF16),
            pltpu.SemaphoreType.DMA((CHUNKS,)),
        ],
        compiler_params=params(("arbitrary",)),
        cost_estimate=cost(2 * total * rows * width, 4 * total * wp),
        name="dispatch",
    )(slot_row, tokens)
    after = {}
    if paired:
        shares = gather_shares(base_weight, 2)
        after = shares["after"]
        pair = swap(for_pair(tokens, grad_out), "tenant")
        after["third"].append(pair)
    got_tokens = exchange(held(send_tokens, [got_grads] + after.get("first", [])))

    back_first, back_second, rank_rows, mask_rows = call(
        functools.partial(back_kernel, cap),
        out_shape=(
            in_hbm((total, split), BF16),
            in_hbm((total, rest + np_), BF16),
            in_hbm((total, ranks), BF16),
            in_hbm((total, ranks), BF16),
        ),
        grid=(steps,),
        in_specs=[
            pl.BlockSpec((devices // steps, height, np_), lambda i: (i, 0, 0)),
            whole((ranks, narrow)),
            any_spec,
        ],
        out_specs=(
            pl.BlockSpec((part, split), lambda i: (i, 0)),
            pl.BlockSpec((part, rest + np_), lambda i: (i, 0)),
            pl.BlockSpec((part, ranks), lambda i: (i, 0)),
            pl.BlockSpec((part, ranks), lambda i: (i, 0)),
        ),
        scratch_shapes=[
            pltpu.VMEM((CHUNKS * ranks, wp), BF16),
            pltpu.SemaphoreType.DMA((CHUNKS,)),
        ],
        compiler_params=params(("arbitrary",)),
        cost_estimate=cost(2 * total * ranks * width, 2 * (total * wp + ranks * width)),
        name="rank_grad_back",
    )(got_grads, right_factor, left_factor)
    rank_rows, mask_rows = hbm(rank_rows, mask_rows)
    got_back = exchange(held(back_first, after.get("third", [])))

    back_second, low_rows = call(
        functools.partial(forth_kernel, cap),
        out_shape=(
            in_hbm((total, rest + np_), BF16),
            in_hbm((total, ranks), BF16),
        ),
        grid=(steps,),
        in_specs=[
            pl.BlockSpec((part, wp), lambda i: (i, 0)),
            pl.BlockSpec((part, ranks), lambda i: (i, 0)),
            any_spec,
            whole((ranks, narrow)),
            any_spec,
        ],
        out_specs=(
            pl.BlockSpec((part, np_), lambda i: (i, rest // np_)),
            pl.BlockSpec((part, ranks), lambda i: (i, 0)),
        ),
        scratch_shapes=[
            pltpu.VMEM((CHUNKS * ranks, wp), BF16),
            pltpu.SemaphoreType.DMA((CHUNKS,)),
        ],
        input_output_aliases={4: 0},
        compiler_params=params(("arbitrary",)),
        cost_estimate=cost(2 * total * ranks * width, 2 * (total * wp + ranks * width)),
        name="lowrank_out",
    )(got_tokens, mask_rows, left_factor, right_factor, hbm(back_second))
    low_rows = hbm(low_rows)
    fourth = shares["last"]([low_rows]) if paired else []
    got_rest = exchange(held(back_second, fourth))

    if paired:
        base_out, base_mine, base_pair = paired_base(
            tokens, grad_out, held(pair, [low_rows]), shares, fsdp_size, 2
        )
    else:
        base_out, base_mine = whole_base(tokens, grad_out, base_weight)
        base_pair = base_mine
    outs = [base_out] + ([base_pair] if paired else [])

    grad_a, grad_b = call(
        functools.partial(page_grad_kernel, cap),
        in_specs=[pl.BlockSpec(memory_space=pltpu.VMEM)] * 4,
        out_shape=(
            in_hbm((ranks, width), BF16),
            in_hbm((ranks, narrow), BF16),
        ),
        compiler_params=params(),
        cost_estimate=cost(2 * total * ranks * width, 2 * (total * wp + ranks * width)),
        name="page_grads",
    )(got_tokens, got_grads, low_rows, rank_rows)

    combine_cost = cost(rows * total * width, total * wp + 4 * rows * width)

    def combine_scratch(cols, extra):
        return [
            pltpu.VMEM((CHUNKS, rows, cols), BF16),
            pltpu.SemaphoreType.DMA((CHUNKS,)),
            pltpu.VMEM((CHUNKS, rows, cols), F32),
            pltpu.SemaphoreType.DMA((CHUNKS,)),
            pltpu.VMEM((devices, block, cols + extra), BF16),
            pltpu.VMEM((rows, rows), F32),
            pltpu.SemaphoreType.DMA((7,)),
        ]

    grad_tokens = call(
        functools.partial(combine_kernel, cap, 0, 0),
        out_shape=in_hbm((rows, width), BF16),
        in_specs=[smem] + [any_spec] * 4,
        out_specs=any_spec,
        scratch_shapes=combine_scratch(split, 0),
        compiler_params=params(),
        cost_estimate=combine_cost,
        name="combine_first",
    )(which, slot_col, hbm(got_back.reshape(devices, block, split)), base_mine, base_pair)
    projected, grad_tokens = call(
        functools.partial(combine_kernel, cap, split, len(outs)),
        out_shape=(in_hbm((rows, narrow), BF16), in_hbm((rows, width), BF16)),
        in_specs=[smem] + [any_spec] * (5 + len(outs)),
        out_specs=(pl.BlockSpec(memory_space=pltpu.VMEM), any_spec),
        scratch_shapes=combine_scratch(rest, np_)
        + [pltpu.VMEM((rows, narrow), F32) for _ in outs],
        input_output_aliases={5 + len(outs): 1},
        compiler_params=params(),
        cost_estimate=combine_cost,
        name="combine_rest",
    )(
        which,
        slot_col,
        hbm(got_rest.reshape(devices, block, rest + np_)),
        base_mine,
        base_pair,
        *outs,
        hbm(grad_tokens),
    )

    return projected, grad_tokens, grad_a[None], grad_b[None]


def solution(mesh):
    rows = P(("groups", "fsdp", "tenant"), None)
    pages = P(("groups", "fsdp", "tenant"), None, None)
    return jax.shard_map(
        on_device,
        mesh=mesh,
        in_specs=(
            rows,
            rows,
            P("fsdp", None),
            pages,
            pages,
            P("groups"),
            P(("groups", "fsdp", "tenant")),
        ),
        out_specs=(rows, rows, pages, pages),
        check_vma=False,
    )
```

```python
import functools

import jax
import jax.numpy as jnp
from jax import lax
from jax.experimental import pallas as pl
from jax.experimental.pallas import tpu as pltpu
from jax.sharding import PartitionSpec as P

RANK = 32
CHUNKS = 8
FIRST = 4
VMEM_LIMIT = 60 * 1024 * 1024

adapter_scale = 2.0

F32 = jnp.float32
BF16 = jnp.bfloat16
NT = (((1,), (1,)), ((), ()))
TN = (((0,), (0,)), ((), ()))


def iota(shape, dim):
    return lax.broadcasted_iota(jnp.int32, shape, dim)


def piece_and_slot(index, cap):
    piece = jnp.zeros_like(index)
    for k in range(1, CHUNKS + 1):
        piece = piece + (index >= k * cap).astype(jnp.int32)
    return piece, index - piece * cap


def spread_mask(rows, cap, lanes):
    block = CHUNKS * cap
    piece, _ = piece_and_slot(iota((block, CHUNKS * lanes), 0), cap)
    group = jnp.zeros_like(piece)
    lane = iota(piece.shape, 1)
    for k in range(1, CHUNKS):
        group = group + (lane >= k * lanes).astype(jnp.int32)
    mask = (piece == group).astype(F32).astype(BF16)
    return jnp.concatenate([mask] * (rows // block), axis=0)


def spread(rows, cap):
    return jnp.concatenate([rows] * CHUNKS, axis=1) * spread_mask(
        rows.shape[0], cap, rows.shape[1]
    )


def pick_piece(wide, cap, lanes):
    block, n = CHUNKS * cap, wide.shape[0]
    piece, _ = piece_and_slot(iota((block, lanes), 0), cap)
    piece = jnp.concatenate([piece] * (n // block), axis=0)
    total = jnp.zeros((n, lanes), F32)
    for k in range(CHUNKS):
        total = total + jnp.where(piece == k, wide[:, k * lanes : (k + 1) * lanes], 0.0)
    return total


def same_slot(cap):
    shape = (CHUNKS * cap, CHUNKS * cap)
    _, slot = piece_and_slot(iota(shape, 0), cap)
    _, slot_c = piece_and_slot(iota(shape, 1), cap)
    return (slot == slot_c).astype(F32)


def fold_pieces(fold, part):
    terms, left = [], part
    for _ in range(3):
        terms.append(left.astype(BF16))
        left = left - terms[-1].astype(F32)
    wide = jnp.dot(
        fold.astype(BF16), jnp.concatenate(terms, axis=1), preferred_element_type=F32
    )
    n = part.shape[1]
    return wide[:, 0:n] + (wide[:, n : 2 * n] + wide[:, 2 * n :])


def load_pieces(src, dst, sem, height, stride, start, width):
    return [
        pltpu.make_async_copy(
            src.at[:, pl.ds(k * stride + start, width)],
            dst.at[pl.ds(k * height, height), pl.ds(0, width)],
            sem.at[k],
        )
        for k in range(CHUNKS)
    ]


def start_all(copies):
    for copy in copies:
        copy.start()


def wait_all(copies):
    for copy in copies:
        copy.wait()


def rows_of_slots(slot, cap, first, group):
    _, slot_of = piece_and_slot(iota((CHUNKS * cap, slot.shape[1]), 0), cap)
    return jnp.concatenate(
        [
            (slot == (slot_of + (first + d) * cap).astype(F32)).astype(F32).astype(BF16)
            for d in range(group)
        ],
        axis=0,
    )


def earlier_rows(rows):
    return (iota((rows, rows), 0) < iota((rows, rows), 1)).astype(F32).astype(BF16)


def grad_pieces(ref, block):
    return jnp.concatenate([ref[d, 0:block, :] for d in range(ref.shape[0])], axis=0)


def route_kernel(
    devices, cap, per_page, owner_ref, tenant_ref, grads_ref, send_ref, row_ref, col_ref
):
    rows = tenant_ref.shape[1]
    height, lanes = send_ref.shape[1:]
    block = CHUNKS * cap
    page = tenant_ref[...] // per_page
    member = tenant_ref[...] - page * per_page

    def add_page(p, target):
        return target + jnp.where(page == p, owner_ref[p], 0)

    target = lax.fori_loop(0, owner_ref.shape[0], add_page, jnp.zeros_like(page))
    chosen = (iota((devices, rows), 0) == target).astype(F32)
    before = jnp.dot(chosen.astype(BF16), earlier_rows(rows), preferred_element_type=F32)
    slot = target.astype(F32) * cap + jnp.sum(before * chosen, axis=0, keepdims=True)
    row_ref[...] = slot
    col_ref[...] = jnp.transpose(jnp.broadcast_to(slot, (rows, rows)))

    pieces = jnp.concatenate(
        [grads_ref[:, k * lanes : (k + 1) * lanes] for k in range(CHUNKS)], axis=0
    )
    here = spread(rows_of_slots(slot, cap, 0, devices), cap)
    packed = jnp.dot(here, pieces, preferred_element_type=F32).astype(BF16)
    of_member = (iota((lanes, rows), 0) // RANK == member).astype(F32).astype(BF16)
    tail = iota((height - block, rows), 0)
    tail = jnp.where(tail < cap, tail, -(10**6))
    in_slot = jnp.concatenate(
        [(slot == (tail + d * cap).astype(F32)).astype(F32).astype(BF16) for d in range(devices)],
        axis=0,
    )
    masks = lax.dot_general(in_slot, of_member, NT, preferred_element_type=F32).astype(BF16)
    extra = height - block
    for d in range(devices):
        send_ref[d, 0:block, :] = packed[d * block : (d + 1) * block, :]
        send_ref[d, block:, :] = masks[d * extra : (d + 1) * extra, :]


def dispatch_kernel(cap, slot_ref, tokens_ref, out_ref, pieces, sem):
    step = pl.program_id(0)
    rows, width = slot_ref.shape[1], pieces.shape[1]
    group = out_ref.shape[0] // (CHUNKS * cap)

    @pl.when(step == 0)
    def _():
        copies = load_pieces(tokens_ref, pieces, sem, rows, width, 0, width)
        start_all(copies)
        wait_all(copies)

    here = rows_of_slots(slot_ref[...], cap, step * group, group)
    out_ref[...] = jnp.dot(spread(here, cap), pieces[...], preferred_element_type=F32).astype(BF16)


def back_kernel(
    cap, got_ref, b_ref, a_ref, first_ref, second_ref, rank_ref, mask_ref, pieces, sem
):
    step = pl.program_id(0)
    ranks = b_ref.shape[0]
    group, height, width = got_ref.shape
    block = CHUNKS * cap
    split = first_ref.shape[1]
    rest = pieces.shape[1] - split
    copies = load_pieces(a_ref, pieces, sem, ranks, split + rest, 0, split + rest)

    @pl.when(step == 0)
    def _():
        start_all(copies)

    tail = height - block
    _, slot = piece_and_slot(iota((block, tail), 0), cap)
    pick_mask = (iota((block, tail), 1) == slot).astype(F32).astype(BF16)
    b_pieces = jnp.concatenate(
        [b_ref[:, k * width : (k + 1) * width] for k in range(CHUNKS)], axis=0
    )
    wide = lax.dot_general(
        grad_pieces(got_ref, block), b_pieces, NT, preferred_element_type=F32
    )
    part = pick_piece(wide, cap, ranks)
    fold = same_slot(cap)
    ranks_of = []
    for d in range(group):
        at = slice(d * block, (d + 1) * block)
        full = fold_pieces(fold, part[at, :])
        mask = jnp.dot(pick_mask, got_ref[d, block:, :], preferred_element_type=F32)
        ranks_of.append((full * mask).astype(BF16))
        mask_ref[at, :] = mask.astype(BF16)
    rank_rows = jnp.concatenate(ranks_of, axis=0)
    rank_ref[...] = rank_rows

    @pl.when(step == 0)
    def _():
        wait_all(copies)

    back = (
        adapter_scale * jnp.dot(spread(rank_rows, cap), pieces[...], preferred_element_type=F32)
    ).astype(BF16)
    first_ref[...] = back[:, 0:split]
    second_ref[:, 0:rest] = back[:, split:]
    second_ref[:, rest:] = jnp.zeros((second_ref.shape[0], second_ref.shape[1] - rest), BF16)


def forth_kernel(
    cap, tok_ref, mask_ref, a_ref, b_ref, _, out_ref, rank_ref, pieces, sem
):
    step = pl.program_id(0)
    ranks = b_ref.shape[0]
    block = CHUNKS * cap
    width = out_ref.shape[1]
    wide_piece = pieces.shape[1]
    group = tok_ref.shape[0] // block

    @pl.when(step == 0)
    def _():
        copies = load_pieces(a_ref, pieces, sem, ranks, wide_piece, 0, wide_piece)
        start_all(copies)
        wait_all(copies)

    b_pieces = jnp.concatenate(
        [b_ref[:, k * width : (k + 1) * width] for k in range(CHUNKS)], axis=0
    )
    wide = lax.dot_general(tok_ref[...], pieces[...], NT, preferred_element_type=F32)
    part = pick_piece(wide, cap, ranks)
    fold = same_slot(cap)
    full = jnp.concatenate(
        [
            fold_pieces(fold, part[d * block : (d + 1) * block, :])
            for d in range(group)
        ],
        axis=0,
    )
    rank_rows = (full * mask_ref[...].astype(F32)).astype(BF16)
    rank_ref[...] = rank_rows
    out_ref[...] = (
        adapter_scale * jnp.dot(spread(rank_rows, cap), b_pieces, preferred_element_type=F32)
    ).astype(BF16)


def page_grad_kernel(cap, tok_ref, grad_ref, low_ref, rank_ref, ga_ref, gb_ref):
    ranks = rank_ref.shape[1]
    wide, narrow = tok_ref.shape[1], grad_ref.shape[2]
    left = lax.dot_general(
        spread(rank_ref[...], cap), tok_ref[...], TN, preferred_element_type=F32
    )
    grads = grad_pieces(grad_ref, CHUNKS * cap)
    right = lax.dot_general(spread(low_ref[...], cap), grads, TN, preferred_element_type=F32)
    for k in range(CHUNKS):
        at = slice(k * ranks, (k + 1) * ranks)
        ga_ref[:, k * wide : (k + 1) * wide] = (adapter_scale * left[at, :]).astype(BF16)
        gb_ref[:, k * narrow : (k + 1) * narrow] = (adapter_scale * right[at, :]).astype(BF16)


def pair_kernel(other_ref, tokens_ref, grads_ref, out_ref, sem):
    rows, narrow = grads_ref.shape
    half = (out_ref.shape[1] - narrow) // CHUNKS
    at = pl.multiple_of(other_ref[0] * half, half)
    copies = [
        pltpu.make_async_copy(
            tokens_ref.at[:, pl.ds(2 * k * half + at, half)],
            out_ref.at[:, pl.ds(k * half, half)],
            sem.at[k],
        )
        for k in range(CHUNKS)
    ]
    copies.append(
        pltpu.make_async_copy(
            grads_ref, out_ref.at[:, pl.ds(CHUNKS * half, narrow)], sem.at[CHUNKS]
        )
    )
    start_all(copies)
    wait_all(copies)


def pair_base_kernel(at_ref, tok_ref, grad_ref, pair_ref, *refs):
    weights, (out_ref, back_ref, theirs_ref) = refs[:-3], refs[-3:]
    rows, narrow = grad_ref.shape
    half_width = back_ref.shape[1]
    grads = jnp.concatenate([grad_ref[...], pair_ref[:, half_width:]], axis=0)
    total = jnp.zeros((2 * rows, narrow), F32)
    share = 2 * half_width // at_ref.shape[0]
    parts = [ref.at[pl.ds(r, share), :] for ref in weights for r in range(0, ref.shape[0], share)]
    for n, ref in enumerate(parts):
        weight = ref[...]
        full = pl.multiple_of(at_ref[2 * n] * share, share)
        part = pl.multiple_of(at_ref[2 * n + 1] * share, share)
        toks = jnp.concatenate(
            [tok_ref[:, pl.ds(full, share)], pair_ref[:, pl.ds(part, share)]], axis=0
        )
        total = total + jnp.dot(toks, weight, preferred_element_type=F32)
        back = lax.dot_general(grads, weight, NT, preferred_element_type=F32)
        back_ref[:, pl.ds(part, share)] = back[0:rows, :]
        theirs_ref[:, pl.ds(part, share)] = back[rows:, :]
    out_ref[...] = total[0:rows, :]
    theirs_ref[:, half_width:] = total[rows:, :]


def base_kernel(tok_ref, grad_ref, w_ref, out_ref, back_ref):
    @pl.when(pl.program_id(0) == 0)
    def _():
        out_ref[...] = jnp.zeros_like(out_ref)

    weight = w_ref[...]
    out_ref[...] += jnp.dot(tok_ref[...], weight, preferred_element_type=F32)
    back_ref[...] = lax.dot_general(grad_ref[...], weight, NT, preferred_element_type=F32)


def combine_kernel(cap, start, extra, which_ref, col_hbm, got_hbm, mine_ref, pair_ref, *refs):
    extras, refs = refs[:extra], refs[extra:]
    if extra:
        projected_ref, refs = refs[1], refs[2:]
    out_hbm, out, sem, base, base_sem, got_ref, col_ref, in_sem, *sums = refs
    devices, block, width = got_ref.shape
    cols = out.shape[2]
    piece = out_hbm.shape[1] // CHUNKS
    parts = 2 if mine_ref.shape[1] < out_hbm.shape[1] else 1
    size = piece // parts
    group = devices // 4 if devices % 4 == 0 else devices

    loads = [pltpu.make_async_copy(col_hbm, col_ref, in_sem.at[0])]
    for n in range(devices // group):
        at = pl.ds(n * group, group)
        loads.append(pltpu.make_async_copy(got_hbm.at[at], got_ref.at[at], in_sem.at[1 + n]))
    late = []
    for n, ref in enumerate(sums):
        last = pl.ds(extras[n].shape[1] - ref.shape[1], ref.shape[1])
        late.append(pltpu.make_async_copy(extras[n].at[:, last], ref, in_sem.at[5 + n]))

    def load(ref, part):
        low, high = max(start, part * size), min(start + cols, (part + 1) * size)
        if low < high:
            start_all(
                [
                    pltpu.make_async_copy(
                        ref.at[:, pl.ds(k * size + low - part * size, high - low)],
                        base.at[k, :, pl.ds(low - start, high - low)],
                        base_sem.at[k],
                    )
                    for k in range(CHUNKS)
                ]
            )

    start_all(loads)
    if parts == 1:
        load(mine_ref, 0)
    else:
        for n in range(2):

            @pl.when(which_ref[0] == n)
            def _():
                load(mine_ref, n)
                load(pair_ref, 1 - n)

    start_all(late)
    wait_all(loads)
    col, rows = col_ref[:, 0:1], col_ref.shape[0]
    copies = []
    for k in range(0, CHUNKS, 2):
        low = k * cap // 16 * 16
        high = min(-(-(k + 2) * cap // 16) * 16, block)
        count = high - low
        lane = iota((1, devices * count), 1)
        row = jnp.zeros_like(lane)
        for d in range(1, devices):
            row = row + (lane >= d * count).astype(jnp.int32)
        slot = lane - row * count + low
        here = []
        for n in (k, k + 1):
            mine = (slot >= n * cap) & (slot < (n + 1) * cap)
            key = jnp.where(mine, row * cap + slot - n * cap, -1).astype(F32)
            here.append((col == key).astype(F32).astype(BF16))
        packed = jnp.concatenate([got_ref[d, low:high, :] for d in range(devices)], axis=0)
        both = jnp.dot(jnp.concatenate(here, axis=0), packed, preferred_element_type=F32)
        for n in (k, k + 1):
            back = both[(n - k) * rows : (n - k + 1) * rows, :]
            pltpu.make_async_copy(base.at[n], base.at[n], base_sem.at[n]).wait()
            out[n] = (base[n] + back[:, 0:cols]).astype(BF16)
            copy = pltpu.make_async_copy(
                out.at[n], out_hbm.at[:, pl.ds(n * piece + start, cols)], sem.at[n]
            )
            copy.start()
            copies.append(copy)
            if extra:
                if n == 0:
                    wait_all(late)
                at = slice(n * (width - cols), (n + 1) * (width - cols))
                total = sum(ref[:, at] for ref in sums) + back[:, cols:]
                projected_ref[:, at] = total.astype(BF16)
    wait_all(copies)


def call(kernel, deps=(), **options):
    specs = list(options.pop("in_specs"))
    count, extra = len(specs), len(deps)

    def body(*refs):
        kernel(*refs[:count], *refs[count + extra :])

    run = pl.pallas_call(
        body, in_specs=specs + [pl.BlockSpec(memory_space=pl.ANY)] * extra, **options
    )
    return lambda *args: run(*args, *deps)


def hbm(*arrays):
    kept = tuple(pltpu.with_memory_space_constraint(x, pltpu.HBM) for x in arrays)
    return kept if len(kept) > 1 else kept[0]


def held(x, deps):
    deps = tuple(deps)
    if not deps:
        return x
    any_spec = pl.BlockSpec(memory_space=pl.ANY)
    return call(
        lambda x_ref, out_ref: None,
        deps=deps,
        out_shape=in_hbm(x.shape, x.dtype),
        in_specs=[any_spec],
        out_specs=any_spec,
        input_output_aliases={0: 0},
        compiler_params=params(),
        cost_estimate=cost(0, 0),
        name="held",
    )(x)


def pick_kernel(count, which_ref, *refs):
    for n in range(count):

        @pl.when(which_ref[0] == n)
        def _():
            refs[count][...] = refs[n][...]


def pick(which, *arrays):
    x = arrays[0]
    return call(
        functools.partial(pick_kernel, len(arrays)),
        out_shape=in_hbm(x.shape, x.dtype),
        in_specs=[pl.BlockSpec(memory_space=pltpu.SMEM)]
        + [pl.BlockSpec(memory_space=pltpu.VMEM)] * len(arrays),
        out_specs=pl.BlockSpec(memory_space=pltpu.VMEM),
        compiler_params=params(),
        cost_estimate=cost(0, 2 * x.size * x.dtype.itemsize),
        name="pick",
    )(which.astype(jnp.int32).reshape(1), *arrays)


def in_hbm(shape, dtype):
    return pltpu.HBM(shape, dtype)


def whole(shape):
    return pl.BlockSpec(shape, lambda *_: (0,) * len(shape))


def params(semantics=None):
    return pltpu.CompilerParams(vmem_limit_bytes=VMEM_LIMIT, dimension_semantics=semantics)


def cost(flops, nbytes):
    return pl.CostEstimate(flops=1, bytes_accessed=1, transcendentals=0)


def swap(x, axis):
    size = lax.axis_size(axis)
    return lax.ppermute(x, axis, [(i, i ^ 1) for i in range(size)])


def gather_shares(base_weight, inner):
    count = lax.axis_size("fsdp")
    z = lax.axis_index("fsdp") // inner
    share = base_weight.shape[0] // 4
    at = lax.axis_index("tenant") * 2 + lax.axis_index("groups")
    mine = lax.dynamic_slice_in_dim(base_weight, at * share, share, 0)

    up_pairs = [(i, i + inner) for i in range(count - inner)]
    up, down = [mine], [mine]
    for j in range(1, 4):
        moved = [p for p in up_pairs if p[0] // inner >= j - 1]
        up.append(lax.ppermute(up[-1], "fsdp", moved))
        moved = [(b, a) for a, b in up_pairs if b // inner <= 4 - j]
        down.append(lax.ppermute(down[-1], "fsdp", moved))

    def of_z(*values):
        return functools.reduce(
            lambda rest, k: jnp.where(z == k, values[k], rest), range(3), values[3]
        )

    held_shares = [
        (mine, [z]),
        (pick(of_z(0, 1, 1, 1), down[1], up[1]), [of_z(1, 0, 1, 2)]),
        (pick(of_z(0, 1, 1, 2), down[2], down[1], up[2]), [of_z(2, 2, 3, 1)]),
        (pick(of_z(0, 1, 2, 3), down[3], down[2], up[2], up[3]), [of_z(3, 3, 0, 0)]),
    ]
    blocks, y_of, x_of, both_of = [], [], [], []

    def spread_share(n, deps=()):
        own, place = held_shares[n]
        y_of.append(held(swap(own, "fsdp"), deps))
        x_of.append(swap(own, "groups"))
        both_of.append(swap(y_of[n], "groups"))
        blocks.extend(
            [
                (own, place, 0, 0),
                (y_of[n], place, 1, 0),
                (x_of[n], place, 0, 1),
                (both_of[n], place, 1, 1),
            ]
        )

    for n in range(3):
        spread_share(n)
    after = {
        "first": [up[2], down[2], y_of[0], x_of[0]],
        "third": [up[3], down[3], y_of[1], x_of[1], both_of[0], y_of[2], x_of[2], both_of[1]],
    }

    def last(deps):
        spread_share(3, deps)
        return [y_of[3], x_of[3]]

    return {"blocks": blocks, "after": after, "last": last}


def for_pair(tokens, grad_out):
    rows, width = tokens.shape
    narrow = grad_out.shape[1]
    any_spec = pl.BlockSpec(memory_space=pl.ANY)
    other = (1 - lax.axis_index("tenant")).astype(jnp.int32).reshape(1)
    return call(
        pair_kernel,
        out_shape=in_hbm((rows, width // 2 + narrow), BF16),
        in_specs=[pl.BlockSpec(memory_space=pltpu.SMEM), any_spec, any_spec],
        out_specs=pl.BlockSpec(memory_space=pltpu.VMEM),
        scratch_shapes=[pltpu.SemaphoreType.DMA((CHUNKS + 1,))],
        compiler_params=params(),
        cost_estimate=cost(0, 4 * rows * (width // 2 + narrow)),
        name="for_pair",
    )(other, tokens, grad_out)


def paired_base(tokens, grad_out, pair, shares, fsdp_size, inner):
    rows, width = tokens.shape
    narrow = grad_out.shape[1]
    tenant, group = lax.axis_index("tenant"), lax.axis_index("groups")
    fsdp = lax.axis_index("fsdp")
    y = fsdp % inner
    gathered = shares["blocks"]
    any_spec = pl.BlockSpec(memory_space=pl.ANY)
    vmem = pl.BlockSpec(memory_space=pltpu.VMEM)
    smem = pl.BlockSpec(memory_space=pltpu.SMEM)

    half = width // 2
    at = []
    for _, places, dy, dx in gathered:
        for place in places:
            shard = place * inner + (y ^ dy)
            x = group ^ dx
            at += [shard * 4 + tenant * 2 + x, shard * 2 + x]
    out, back, theirs = call(
        pair_base_kernel,
        out_shape=(
            in_hbm((rows, narrow), F32),
            in_hbm((rows, half), F32),
            in_hbm((rows, half + narrow), F32),
        ),
        in_specs=[smem] + [vmem] * (3 + len(gathered)),
        out_specs=(vmem, vmem, vmem),
        compiler_params=params(),
        cost_estimate=cost(4 * rows * width * narrow, width * narrow),
        name="base",
    )(jnp.stack(at).astype(jnp.int32), tokens, grad_out, pair, *[g[0] for g in gathered])
    theirs = swap(theirs, "tenant")
    return hbm(out), hbm(back), hbm(theirs)


def whole_base(tokens, grad_out, base_weight):
    rows, width = tokens.shape
    narrow = grad_out.shape[1]
    wp = width // CHUNKS
    group_size, tenant_size = lax.axis_size("groups"), lax.axis_size("tenant")
    shares = group_size * tenant_size
    share = base_weight.shape[0] // shares
    which = lax.axis_index("groups") * tenant_size + lax.axis_index("tenant")
    mine = lax.dynamic_slice_in_dim(base_weight, which * share, share, 0)
    weight = lax.all_gather(mine, ("fsdp", "groups", "tenant"), axis=0, tiled=True)
    return call(
        base_kernel,
        out_shape=(
            in_hbm((rows, narrow), F32),
            in_hbm((rows, width), F32),
        ),
        grid=(CHUNKS,),
        in_specs=[
            pl.BlockSpec((rows, wp), lambda i: (0, i)),
            whole((rows, narrow)),
            pl.BlockSpec((wp, narrow), lambda i: (i, 0)),
        ],
        out_specs=(whole((rows, narrow)), pl.BlockSpec((rows, wp), lambda i: (0, i))),
        compiler_params=params(("arbitrary",)),
        cost_estimate=cost(4 * rows * width * narrow, 2 * width * narrow),
        name="base",
    )(tokens, grad_out, weight)


def on_device(tokens, grad_out, base_weight, page_a, page_b, page_owner, row_tenant):
    rows, width = tokens.shape
    narrow = grad_out.shape[1]
    fsdp_size = lax.axis_size("fsdp")
    tenant_size = lax.axis_size("tenant")
    devices = fsdp_size * tenant_size
    cap = max(4, 4 * rows // (3 * devices))
    per_page = page_a.shape[1] // RANK
    ranks = page_a.shape[1]
    block = CHUNKS * cap
    total = devices * block
    wp, np_ = width // CHUNKS, narrow // CHUNKS
    split = wp // 128 * FIRST // 8 * 128
    rest = wp - split
    height = block + -(-cap // 16) * 16
    left_factor, right_factor = hbm(page_a[0], page_b[0])
    tokens, grad_out = hbm(tokens, grad_out)
    axes = ("fsdp", "tenant")
    which = lax.axis_index("tenant").astype(jnp.int32).reshape(1)

    def exchange(x):
        return lax.all_to_all(x, axes, split_axis=0, concat_axis=0, tiled=True)

    any_spec = pl.BlockSpec(memory_space=pl.ANY)
    smem = pl.BlockSpec(memory_space=pltpu.SMEM)
    paired = (
        fsdp_size == 8
        and tenant_size == 2
        and lax.axis_size("groups") == 2
        and width // fsdp_size == wp
    )

    steps = 4 if devices % 4 == 0 else 1
    send_grads, slot_row, slot_col = call(
        functools.partial(route_kernel, devices, cap, per_page),
        out_shape=(
            in_hbm((devices, height, np_), BF16),
            in_hbm((1, rows), F32),
            in_hbm((rows, rows), F32),
        ),
        in_specs=[smem] + [pl.BlockSpec(memory_space=pltpu.VMEM)] * 2,
        out_specs=tuple(pl.BlockSpec(memory_space=pltpu.VMEM) for _ in range(3)),
        compiler_params=params(),
        cost_estimate=cost(2 * total * rows * narrow, 4 * total * np_),
        name="route",
    )(page_owner, row_tenant.reshape(1, rows), grad_out)
    slot_row, slot_col = hbm(slot_row, slot_col)
    got_grads = exchange(send_grads)

    steps = 4 if devices % 4 == 0 else 1
    part = total // steps
    send_tokens = call(
        functools.partial(dispatch_kernel, cap),
        out_shape=in_hbm((total, wp), BF16),
        grid=(steps,),
        in_specs=[whole((1, rows)), any_spec],
        out_specs=pl.BlockSpec((part, wp), lambda i: (i, 0)),
        scratch_shapes=[
            pltpu.VMEM((CHUNKS * rows, wp), BF16),
            pltpu.SemaphoreType.DMA((CHUNKS,)),
        ],
        compiler_params=params(("arbitrary",)),
        cost_estimate=cost(2 * total * rows * width, 4 * total * wp),
        name="dispatch",
    )(slot_row, tokens)
    after = {}
    if paired:
        shares = gather_shares(base_weight, 2)
        after = shares["after"]
        pair = for_pair(tokens, grad_out)
        after["first"].append(pair)
        pair = swap(pair, "tenant")
        after["third"].append(pair)
    got_tokens = exchange(held(send_tokens, [got_grads] + after.get("first", [])))

    back_first, back_second, rank_rows, mask_rows = call(
        functools.partial(back_kernel, cap),
        out_shape=(
            in_hbm((total, split), BF16),
            in_hbm((total, rest + np_), BF16),
            in_hbm((total, ranks), BF16),
            in_hbm((total, ranks), BF16),
        ),
        grid=(steps,),
        in_specs=[
            pl.BlockSpec((devices // steps, height, np_), lambda i: (i, 0, 0)),
            whole((ranks, narrow)),
            any_spec,
        ],
        out_specs=(
            pl.BlockSpec((part, split), lambda i: (i, 0)),
            pl.BlockSpec((part, rest + np_), lambda i: (i, 0)),
            pl.BlockSpec((part, ranks), lambda i: (i, 0)),
            pl.BlockSpec((part, ranks), lambda i: (i, 0)),
        ),
        scratch_shapes=[
            pltpu.VMEM((CHUNKS * ranks, wp), BF16),
            pltpu.SemaphoreType.DMA((CHUNKS,)),
        ],
        compiler_params=params(("arbitrary",)),
        cost_estimate=cost(2 * total * ranks * width, 2 * (total * wp + ranks * width)),
        name="rank_grad_back",
    )(got_grads, right_factor, left_factor)
    rank_rows, mask_rows = hbm(rank_rows, mask_rows)
    got_back = exchange(held(back_first, after.get("third", [])))

    back_second, low_rows = call(
        functools.partial(forth_kernel, cap),
        out_shape=(
            in_hbm((total, rest + np_), BF16),
            in_hbm((total, ranks), BF16),
        ),
        grid=(steps,),
        in_specs=[
            pl.BlockSpec((part, wp), lambda i: (i, 0)),
            pl.BlockSpec((part, ranks), lambda i: (i, 0)),
            any_spec,
            whole((ranks, narrow)),
            any_spec,
        ],
        out_specs=(
            pl.BlockSpec((part, np_), lambda i: (i, rest // np_)),
            pl.BlockSpec((part, ranks), lambda i: (i, 0)),
        ),
        scratch_shapes=[
            pltpu.VMEM((CHUNKS * ranks, wp), BF16),
            pltpu.SemaphoreType.DMA((CHUNKS,)),
        ],
        input_output_aliases={4: 0},
        compiler_params=params(("arbitrary",)),
        cost_estimate=cost(2 * total * ranks * width, 2 * (total * wp + ranks * width)),
        name="lowrank_out",
    )(got_tokens, mask_rows, left_factor, right_factor, hbm(back_second))
    low_rows = hbm(low_rows)
    fourth = shares["last"]([low_rows]) if paired else []
    got_rest = exchange(held(back_second, fourth))

    if paired:
        base_out, base_mine, base_pair = paired_base(
            tokens, grad_out, held(pair, [low_rows]), shares, fsdp_size, 2
        )
    else:
        base_out, base_mine = whole_base(tokens, grad_out, base_weight)
        base_pair = base_mine
    outs = [base_out] + ([base_pair] if paired else [])

    grad_a, grad_b = call(
        functools.partial(page_grad_kernel, cap),
        in_specs=[pl.BlockSpec(memory_space=pltpu.VMEM)] * 4,
        out_shape=(
            in_hbm((ranks, width), BF16),
            in_hbm((ranks, narrow), BF16),
        ),
        compiler_params=params(),
        cost_estimate=cost(2 * total * ranks * width, 2 * (total * wp + ranks * width)),
        name="page_grads",
    )(got_tokens, got_grads, low_rows, rank_rows)

    combine_cost = cost(rows * total * width, total * wp + 4 * rows * width)

    def combine_scratch(cols, extra):
        return [
            pltpu.VMEM((CHUNKS, rows, cols), BF16),
            pltpu.SemaphoreType.DMA((CHUNKS,)),
            pltpu.VMEM((CHUNKS, rows, cols), F32),
            pltpu.SemaphoreType.DMA((CHUNKS,)),
            pltpu.VMEM((devices, block, cols + extra), BF16),
            pltpu.VMEM((rows, rows), F32),
            pltpu.SemaphoreType.DMA((7,)),
        ]

    grad_tokens = call(
        functools.partial(combine_kernel, cap, 0, 0),
        out_shape=in_hbm((rows, width), BF16),
        in_specs=[smem] + [any_spec] * 4,
        out_specs=any_spec,
        scratch_shapes=combine_scratch(split, 0),
        compiler_params=params(),
        cost_estimate=combine_cost,
        name="combine_first",
    )(which, slot_col, hbm(got_back.reshape(devices, block, split)), base_mine, base_pair)
    projected, grad_tokens = call(
        functools.partial(combine_kernel, cap, split, len(outs)),
        out_shape=(in_hbm((rows, narrow), BF16), in_hbm((rows, width), BF16)),
        in_specs=[smem] + [any_spec] * (5 + len(outs)),
        out_specs=(pl.BlockSpec(memory_space=pltpu.VMEM), any_spec),
        scratch_shapes=combine_scratch(rest, np_)
        + [pltpu.VMEM((rows, narrow), F32) for _ in outs],
        input_output_aliases={5 + len(outs): 1},
        compiler_params=params(),
        cost_estimate=combine_cost,
        name="combine_rest",
    )(
        which,
        slot_col,
        hbm(got_rest.reshape(devices, block, rest + np_)),
        base_mine,
        base_pair,
        *outs,
        hbm(grad_tokens),
    )

    return projected, grad_tokens, grad_a[None], grad_b[None]


def solution(mesh):
    rows = P(("groups", "fsdp", "tenant"), None)
    pages = P(("groups", "fsdp", "tenant"), None, None)
    return jax.shard_map(
        on_device,
        mesh=mesh,
        in_specs=(
            rows,
            rows,
            P("fsdp", None),
            pages,
            pages,
            P("groups"),
            P(("groups", "fsdp", "tenant")),
        ),
        out_specs=(rows, rows, pages, pages),
        check_vma=False,
    )
```
